32 devices in a mesh: grp: 2 (over y), shard: 16 (over z, x, core).
Axes of the slice: x: 2, y: 2, z: 4, core: 2. Of those that a mesh axis runs over, the one named last changes fastest.
Arguments:
- query_rows: bfloat16 [8192, 1024], P(('grp', 'shard')), may hold values from -6 to 6
- key_rows: bfloat16 [8192, 1024], P(('grp', 'shard')), may hold values from -6 to 6
- value_rows: bfloat16 [8192, 1024], P(('grp', 'shard')), may hold values from -6 to 6
- grad_out: bfloat16 [8192, 1024], P(('grp', 'shard')), may hold values from -6 to 6
Outputs:
- attended: bfloat16 [8192, 1024], P(('grp', 'shard'))
- grad_query: bfloat16 [8192, 1024], P(('grp', 'shard'))
- grad_key: bfloat16 [8192, 1024], P(('grp', 'shard'))
- grad_value: bfloat16 [8192, 1024], P(('grp', 'shard'))
The draws below stay inside these ranges and needn't reach their ends.
All inputs are finite; a program needn't handle non-finite values.
Results may differ from the reference program's by a relative error of at most 0.012.
Values may be sent and summed in bfloat16 or wider, within the bound.
No kernel may reach another device: no remote copies, remote signals or barrier semaphores. Data moves between devices by JAX's collectives and lax.ppermute only.
A program may use at most 256 MiB of HBM per device.

```python
import jax
import jax.numpy as jnp
from jax import lax

HEADS = 8
HD = 128
TOK_DEV = 256
TOKENS = 8192


def levels(rng, dims, shards, smallest, top_value):
    loudness = 1.0
    for axis_at, parts in shards:
        draws = jax.random.uniform(jax.random.fold_in(jax.random.fold_in(rng, 6), axis_at), (parts,), jnp.float32, smallest / len(shards), top_value / len(shards))
        loudness = loudness * jnp.repeat(jnp.exp(draws), dims[axis_at] // parts).reshape((-1,) + (1,) * (len(dims) - 1 - axis_at))
    return loudness


def normal_values(stream_key, shape, deviation, limit, shards=(), dtype=jnp.bfloat16):
    result = deviation * jax.random.normal(stream_key, shape, jnp.float32)
    if shards:
        result = result * levels(stream_key, shape, shards, -0.22, 0.18)
    return jnp.clip(result, -limit, limit).astype(dtype)


def setup_inputs(seed: int = 0) -> dict:
    key_list = jax.random.split(jax.random.key(seed), 5)
    return {
        "query_rows": normal_values(key_list[0], (TOKENS, HEADS * HD), 1.0, 6.0, ((0, 32),)),
        "key_rows": normal_values(key_list[1], (TOKENS, HEADS * HD), 1.0, 6.0, ((0, 32),)),
        "value_rows": normal_values(key_list[2], (TOKENS, HEADS * HD), 1.0, 6.0, ((0, 32),)),
        "grad_out": normal_values(key_list[3], (TOKENS, HEADS * HD), 1.0, 6.0, ((0, 32),)),
    }


def rounded(array):
    return lax.optimization_barrier(array.astype(jnp.bfloat16)).astype(jnp.float32)

def causal_mask():
    rows_at = lax.broadcasted_iota(jnp.int32, (TOK_DEV, TOK_DEV), 0)
    cols_at = lax.broadcasted_iota(jnp.int32, (TOK_DEV, TOK_DEV), 1)
    return (rows_at >= cols_at)[None]

def block_scores(query_float, key_float, value_float, grad_float):
    causal = causal_mask()
    scores = jnp.einsum('thd,shd->hts', query_float, key_float)
    local_scores = rounded(jnp.where(causal, scores, 0.0))
    grad_raw = jnp.einsum('the,she->hts', grad_float, value_float)
    grad_scores = rounded(jnp.where(causal, grad_raw, 0.0))
    return (local_scores, grad_scores)

def reference(query_rows, key_rows, value_rows, grad_out):
    seq_len = query_rows.shape[0]
    block_count = seq_len // TOK_DEV

    def split(array):
        return array.reshape(block_count, TOK_DEV, HEADS, HD)
    causal = causal_mask()
    blocks = (split(query_rows), split(key_rows), split(value_rows), split(grad_out))

    def forward_step(carry, pieces):
        query_float = pieces[0].astype(jnp.float32)
        key_float = pieces[1].astype(jnp.float32)
        value_float = pieces[2].astype(jnp.float32)
        grad_float = pieces[3].astype(jnp.float32)
        scores = jnp.einsum('thd,shd->hts', query_float, key_float)
        local_scores = rounded(jnp.where(causal, scores, 0.0))
        block_state = jnp.einsum('thd,the->hde', key_float, value_float)
        earlier_rounded = rounded(carry)
        mixed_rows = jnp.einsum('hts,she->the', local_scores, value_float) + jnp.einsum('thd,hde->the', query_float, earlier_rounded)
        inv_rms = lax.rsqrt(lax.optimization_barrier(jnp.mean(mixed_rows * mixed_rows, axis=-1, keepdims=True)) + 1.0)
        normed = mixed_rows * inv_rms
        attended = normed.astype(jnp.bfloat16)
        grad_mixed = ((grad_float - normed * lax.optimization_barrier(jnp.mean(grad_float * normed, axis=-1, keepdims=True))) * inv_rms).astype(jnp.bfloat16)
        grad_mixed_float = lax.optimization_barrier(grad_mixed).astype(jnp.float32)
        grad_raw = jnp.einsum('the,she->hts', grad_mixed_float, value_float)
        grad_scores = rounded(jnp.where(causal, grad_raw, 0.0))
        grad_query = jnp.einsum('hts,shd->thd', grad_scores, key_float) + jnp.einsum('the,hde->thd', grad_mixed_float, earlier_rounded)
        return (carry + block_state, (attended, grad_query.astype(jnp.bfloat16), grad_mixed))
    start = jnp.zeros((HEADS, HD, HD), jnp.float32)
    unused, outputs = lax.scan(forward_step, start, blocks)
    attended, grad_query, grad_mixed = outputs

    def backward_step(carry, pieces):
        query_float = pieces[0].astype(jnp.float32)
        key_float = pieces[1].astype(jnp.float32)
        value_float = pieces[2].astype(jnp.float32)
        grad_float = pieces[3].astype(jnp.float32)
        local_scores, grad_scores = block_scores(query_float, key_float, value_float, grad_float)
        later_rounded = rounded(carry)
        grad_key = jnp.einsum('hts,thd->shd', grad_scores, query_float) + jnp.einsum('she,hde->shd', value_float, later_rounded)
        grad_value = jnp.einsum('hts,the->she', local_scores, grad_float) + jnp.einsum('shd,hde->she', key_float, later_rounded)
        block_reverse = jnp.einsum('thd,the->hde', query_float, grad_float)
        return (carry + block_reverse, (grad_key.astype(jnp.bfloat16), grad_value.astype(jnp.bfloat16)))
    back_blocks = (blocks[0], blocks[1], blocks[2], grad_mixed)
    unused_back, back_outputs = lax.scan(backward_step, start, back_blocks, reverse=True)
    grad_key, grad_value = back_outputs

    def joined(array):
        return array.reshape(seq_len, HEADS * HD)
    return (joined(attended), joined(grad_query), joined(grad_key), joined(grad_value))
```

```python
import functools

import jax
import jax.numpy as jnp
from jax import lax
from jax.experimental import pallas as pl
from jax.experimental.pallas import tpu as pltpu
from jax.sharding import PartitionSpec as P

HD = 128
AXES = ("grp", "shard")
F32 = jnp.float32
BF16 = jnp.bfloat16


def dot_nn(a, b):
    return lax.dot_general(a, b, (((1,), (0,)), ((), ())), preferred_element_type=F32)


def dot_nt(a, b):
    return lax.dot_general(a, b, (((1,), (1,)), ((), ())), preferred_element_type=F32)


def dot_tn(a, b):
    return lax.dot_general(a, b, (((0,), (0,)), ((), ())), preferred_element_type=F32)


def columns(head):
    start = head * HD
    if not isinstance(head, int):
        start = pl.multiple_of(start, HD)
    return pl.ds(start, HD)


def call(kernel, out_shapes, flops, *args):
    smem = pl.BlockSpec(memory_space=pltpu.SMEM)
    vmem = pl.BlockSpec(memory_space=pltpu.VMEM)
    size = sum(a.size * a.dtype.itemsize for a in (*args, *out_shapes))
    return pl.pallas_call(
        kernel,
        out_shape=out_shapes,
        in_specs=[smem if a.dtype == jnp.int32 else vmem for a in args],
        out_specs=[vmem] * len(out_shapes),
        compiler_params=pltpu.CompilerParams(vmem_limit_bytes=32 * 1024 * 1024),
        cost_estimate=pl.CostEstimate(flops=flops, bytes_accessed=size, transcendentals=0),
    )(*args)


def state_kernel(half, core_ref, k_ref, v_ref, own_ref, send_ref):
    core = core_ref[0]
    for j in range(half):
        cols = columns((1 - core) * half + j)
        send_ref[j] = dot_tn(k_ref[:, cols], v_ref[:, cols]).astype(BF16)
    for j in range(half):
        cols = columns(core * half + j)
        own_ref[j] = dot_tn(k_ref[:, cols], v_ref[:, cols])


def lower(rows):
    return lax.broadcasted_iota(jnp.int32, (rows, rows), 0) >= lax.broadcasted_iota(
        jnp.int32, (rows, rows), 1
    )


def upper(rows):
    return lax.broadcasted_iota(jnp.int32, (rows, rows), 0) <= lax.broadcasted_iota(
        jnp.int32, (rows, rows), 1
    )


def local_kernel(heads, q_ref, k_ref, v_ref, mixed_ref, qt_ref):
    mask = lower(q_ref.shape[0])
    for h in range(heads):
        cols = columns(h)
        q = q_ref[:, cols]
        scores = jnp.where(mask, dot_nt(q, k_ref[:, cols]), 0.0).astype(BF16)
        mixed_ref[:, cols] = dot_nn(scores, v_ref[:, cols])
        qt_ref[h] = q.T


def norm_kernel(half, core_ref, q_ref, g_ref, qt_ref, mixed_ref, eown_ref, eother_ref, att_ref, gm_ref, own_ref, send_ref):
    core = core_ref[0]
    for mine, state_ref in ((0, eother_ref), (1, eown_ref)):
        for j in range(half):
            head = (core if mine else 1 - core) * half + j
            cols = columns(head)
            mixed = mixed_ref[:, cols] + dot_nn(q_ref[:, cols], state_ref[j])
            inv_rms = lax.rsqrt(jnp.mean(mixed * mixed, axis=-1, keepdims=True) + 1.0)
            normed = mixed * inv_rms
            att_ref[:, cols] = normed.astype(BF16)
            g = g_ref[:, cols].astype(F32)
            gm = ((g - normed * jnp.mean(g * normed, axis=-1, keepdims=True)) * inv_rms).astype(BF16)
            gm_ref[:, cols] = gm
            state = dot_nn(qt_ref[head], gm)
            if mine:
                own_ref[j] = state
            else:
                send_ref[j] = state.astype(BF16)


def grads_kernel(half, core_ref, q_ref, k_ref, v_ref, gm_ref, eown_ref, eother_ref, gq_ref, kl_ref, vl_ref):
    core = core_ref[0]
    rows = q_ref.shape[0]
    low = lower(rows)
    upp = upper(rows)
    for mine, state_ref in ((0, eother_ref), (1, eown_ref)):
        for j in range(half):
            cols = columns((core if mine else 1 - core) * half + j)
            q = q_ref[:, cols]
            k = k_ref[:, cols]
            v = v_ref[:, cols]
            gm = gm_ref[:, cols]
            gs = jnp.where(low, dot_nt(gm, v), 0.0).astype(BF16)
            gq_ref[:, cols] = (dot_nn(gs, k) + dot_nt(gm, state_ref[j])).astype(BF16)
            gst = jnp.where(upp, dot_nt(v, gm), 0.0).astype(BF16)
            kl_ref[:, cols] = dot_nn(gst, q)
            lst = jnp.where(upp, dot_nt(k, q), 0.0).astype(BF16)
            vl_ref[:, cols] = dot_nn(lst, gm)


def last_kernel(half, core_ref, k_ref, v_ref, kl_ref, vl_ref, lown_ref, lother_ref, gk_ref, gv_ref):
    core = core_ref[0]
    for mine, state_ref in ((0, lother_ref), (1, lown_ref)):
        for j in range(half):
            cols = columns((core if mine else 1 - core) * half + j)
            later = state_ref[j]
            gk_ref[:, cols] = (kl_ref[:, cols] + dot_nt(v_ref[:, cols], later)).astype(BF16)
            gv_ref[:, cols] = (vl_ref[:, cols] + dot_nn(k_ref[:, cols], later)).astype(BF16)


def swap(array, bit, count):
    return lax.ppermute(array, AXES, [(i, i ^ bit) for i in range(count)])


def scan_states(own, send, place, count, backward):
    def before(bit):
        is_set = (place & bit) != 0
        return ~is_set if backward else is_set

    from_core = swap(send, 1, count).astype(F32)
    total = own + from_core
    entering = jnp.zeros_like(own)
    bit = 2
    while bit < count:
        arrived = swap(total.astype(BF16), bit, count).astype(F32)
        entering = entering + jnp.where(before(bit), arrived, 0.0)
        total = total + arrived
        bit *= 2
    mine = entering + jnp.where(before(1), from_core, 0.0)
    theirs = entering + jnp.where(before(1), 0.0, own)
    return mine.astype(BF16), swap(theirs.astype(BF16), 1, count)


def body(query_rows, key_rows, value_rows, grad_out):
    rows, width = query_rows.shape
    heads = width // HD
    half = heads // 2
    count = lax.axis_size("grp") * lax.axis_size("shard")
    place = lax.axis_index(AXES)
    core = (place & 1).astype(jnp.int32).reshape(1)
    part = jax.ShapeDtypeStruct((half, HD, HD), F32)
    part16 = jax.ShapeDtypeStruct((half, HD, HD), BF16)
    full = jax.ShapeDtypeStruct((rows, width), F32)
    full16 = jax.ShapeDtypeStruct((rows, width), BF16)
    turned = jax.ShapeDtypeStruct((heads, HD, rows), BF16)
    work = 2 * rows * width * HD
    scores = 2 * rows * width * rows

    own, send = call(
        functools.partial(state_kernel, half), (part, part16), work, core, key_rows, value_rows
    )
    e_own, e_other = scan_states(own, send, place, count, False)
    mixed, q_turned = call(
        functools.partial(local_kernel, heads), (full, turned), 2 * scores, query_rows, key_rows, value_rows
    )
    attended, grad_mixed, own, send = call(
        functools.partial(norm_kernel, half),
        (full16, full16, part, part16),
        2 * work,
        core, query_rows, grad_out, q_turned, mixed, e_own, e_other,
    )
    l_own, l_other = scan_states(own, send, place, count, True)
    grad_query, key_local, value_local = call(
        functools.partial(grads_kernel, half),
        (full16, full, full),
        6 * scores + work,
        core, query_rows, key_rows, value_rows, grad_mixed, e_own, e_other,
    )
    grad_key, grad_value = call(
        functools.partial(last_kernel, half),
        (full16, full16),
        2 * work,
        core, key_rows, value_rows, key_local, value_local, l_own, l_other,
    )
    return attended, grad_query, grad_key, grad_value


def solution(mesh):
    spec = P(AXES, None)
    return jax.shard_map(
        body, mesh=mesh, in_specs=(spec,) * 4, out_specs=(spec,) * 4, check_vma=False
    )
```

```python
import functools

import jax
import jax.numpy as jnp
from jax import lax
from jax.experimental import pallas as pl
from jax.experimental.pallas import tpu as pltpu
from jax.sharding import PartitionSpec as P

HD = 128
AXES = ("grp", "shard")
F32 = jnp.float32
BF16 = jnp.bfloat16


def dot(a, b, a_dim, b_dim):
    return lax.dot_general(a, b, (((a_dim,), (b_dim,)), ((), ())), preferred_element_type=F32)


def columns(slot, key):
    return pl.ds(pl.multiple_of((slot ^ key) * HD, HD), HD)


def triangle(rows, keep_lower):
    at_row = lax.broadcasted_iota(jnp.int32, (rows, rows), 0)
    at_col = lax.broadcasted_iota(jnp.int32, (rows, rows), 1)
    return at_row >= at_col if keep_lower else at_row <= at_col


def call(kernel, outs, args, flops, out_hbm=0, in_hbm=(), scratch=(), aliases=None):
    smem = pl.BlockSpec(memory_space=pltpu.SMEM)
    vmem = pl.BlockSpec(memory_space=pltpu.VMEM)
    hbm = pl.BlockSpec(memory_space=pltpu.HBM)
    shapes = [jax.ShapeDtypeStruct(shape, dtype) for shape, dtype in outs]
    size = sum(a.size * a.dtype.itemsize for a in (*args, *shapes))
    specs = [smem if a.dtype == jnp.int32 else hbm if i in in_hbm else vmem for i, a in enumerate(args)]
    return pl.pallas_call(
        kernel,
        out_shape=shapes,
        in_specs=specs,
        out_specs=[hbm if i < out_hbm else vmem for i in range(len(shapes))],
        scratch_shapes=list(scratch),
        input_output_aliases=aliases or {},
        compiler_params=pltpu.CompilerParams(vmem_limit_bytes=32 * 1024 * 1024),
        cost_estimate=pl.CostEstimate(flops=flops, bytes_accessed=size, transcendentals=0),
    )(*args)


def state_kernel(base, key_ref, k_hbm, v_hbm, out_ref, k_buf, v_buf, sems):
    key = key_ref[0]
    copies = []
    for j in range(out_ref.shape[0]):
        cols = columns(base + j, key)
        pair = (
            pltpu.make_async_copy(k_hbm.at[:, cols], k_buf.at[j], sems.at[0, j]),
            pltpu.make_async_copy(v_hbm.at[:, cols], v_buf.at[j], sems.at[1, j]),
        )
        for copy in pair:
            copy.start()
        copies.append(pair)
    for j, pair in enumerate(copies):
        for copy in pair:
            copy.wait()
        out_ref[j] = dot(k_buf[j], v_buf[j], 0, 0).astype(out_ref.dtype)


def local_kernel(key_ref, q_ref, k_ref, v_ref, mixed_ref, turned_ref, scores_ref):
    key = key_ref[0]
    rows = q_ref.shape[0]
    low = triangle(rows, True)
    high = triangle(rows, False)
    for s in range(mixed_ref.shape[0]):
        cols = columns(s, key)
        q = q_ref[:, cols]
        k = k_ref[:, cols]
        scores = jnp.where(low, dot(q, k, 1, 1), 0.0).astype(BF16)
        mixed_ref[s] = dot(scores, v_ref[:, cols], 1, 0)
        turned_ref[s] = q.T
        scores_ref[s] = jnp.where(high, dot(k, q, 1, 1), 0.0).astype(BF16)


def norm_kernel(base, key_ref, q_ref, g_ref, turned_ref, mixed_ref, e_ref, att_ref, gm_ref, state_ref):
    key = key_ref[0]
    for j in range(e_ref.shape[0]):
        cols = columns(base + j, key)
        mixed = mixed_ref[base + j] + dot(q_ref[:, cols], e_ref[j], 1, 0)
        inv_rms = lax.rsqrt(jnp.mean(mixed * mixed, axis=-1, keepdims=True) + 1.0)
        normed = mixed * inv_rms
        att_ref[j] = normed.astype(BF16)
        g = g_ref[:, cols].astype(F32)
        gm = ((g - normed * jnp.mean(g * normed, axis=-1, keepdims=True)) * inv_rms).astype(BF16)
        gm_ref[j] = gm
        state_ref[j] = dot(turned_ref[base + j], gm, 1, 0).astype(state_ref.dtype)


def grads_kernel(base, key_ref, q_ref, k_ref, v_ref, att_ref, gm_ref, e_ref, scores_ref, *refs):
    att_hbm, gq_hbm, kl_ref, vl_ref, gq_buf, sems = refs[-6:]
    key = key_ref[0]
    rows = q_ref.shape[0]
    low = triangle(rows, True)
    high = triangle(rows, False)
    copies = []
    for j in range(e_ref.shape[0]):
        cols = columns(base + j, key)
        copies.append(pltpu.make_async_copy(att_ref.at[j], att_hbm.at[:, cols], sems.at[0, j]))
        copies[-1].start()
        v = v_ref[:, cols]
        gm = gm_ref[j]
        gs = jnp.where(low, dot(gm, v, 1, 1), 0.0).astype(BF16)
        gq_buf[j] = (dot(gs, k_ref[:, cols], 1, 0) + dot(gm, e_ref[j], 1, 1)).astype(BF16)
        copies.append(pltpu.make_async_copy(gq_buf.at[j], gq_hbm.at[:, cols], sems.at[1, j]))
        copies[-1].start()
        gs_turned = jnp.where(high, dot(v, gm, 1, 1), 0.0).astype(BF16)
        kl_ref[j] = dot(gs_turned, q_ref[:, cols], 1, 0)
        vl_ref[j] = dot(scores_ref[base + j], gm, 1, 0)
    for copy in copies:
        copy.wait()


def last_kernel(base, key_ref, k_ref, v_ref, kl_ref, vl_ref, l_ref, *refs):
    gk_hbm, gv_hbm, gk_buf, gv_buf, sems = refs[-5:]
    key = key_ref[0]
    copies = []
    for j in range(l_ref.shape[0]):
        cols = columns(base + j, key)
        later = l_ref[j]
        gk_buf[j] = (kl_ref[j] + dot(v_ref[:, cols], later, 1, 1)).astype(BF16)
        copies.append(pltpu.make_async_copy(gk_buf.at[j], gk_hbm.at[:, cols], sems.at[0, j]))
        copies[-1].start()
        gv_buf[j] = (vl_ref[j] + dot(k_ref[:, cols], later, 1, 0)).astype(BF16)
        copies.append(pltpu.make_async_copy(gv_buf.at[j], gv_hbm.at[:, cols], sems.at[1, j]))
        copies[-1].start()
    for copy in copies:
        copy.wait()


def swap(array, mask, count):
    return lax.ppermute(array, AXES, [(i, i ^ mask) for i in range(count)])


def exchange_levels(count):
    bits = count.bit_length() - 1
    levels = []
    bit = 3
    while bit < bits:
        first = (1 << bit) | 1
        if bit + 1 < bits:
            second = 1 << (bit + 1)
            levels.append((first | second, second, first))
        else:
            levels.append((first,))
        bit += 2
    return levels


SCATTER = (3, 4, 7)


def slot_key(place, count):
    bits = count.bit_length() - 1
    half = (place ^ (place >> 1)) & 1
    for bit in range(3, bits, 2):
        half = half ^ ((place >> bit) & 1)
    return (half << 2) | ((place >> 1) & 3)


def beside(arrays, work, tie):
    if work is None:
        return arrays, None
    done = work(tie)
    return lax.optimization_barrier((arrays, done))


def scan_states(own, from_core, place, count, backward, works):
    def before(a, b):
        return (a > b) if backward else (a < b)

    def pick(condition, array):
        return jnp.where(condition, array, 0.0)

    chip = place >> 1
    total = own + from_core
    rounded = total.astype(BF16)
    arrived = [swap(rounded[j], SCATTER[j - 1], count) for j in (1, 2, 3)]
    arrived, first = beside(arrived, works[0], rounded)
    parts = [total[0], *(a.astype(F32) for a in arrived)]
    cluster = parts[0] + parts[1] + parts[2] + parts[3]
    entering = jnp.zeros_like(cluster)
    second = None
    for at, masks in enumerate(exchange_levels(count)):
        rounded = cluster.astype(BF16)
        arrived = [swap(rounded, mask, count) for mask in masks]
        if at == 0:
            arrived, second = beside(arrived, works[1], rounded)
        for mask, array in zip(masks, arrived):
            array = array.astype(F32)
            entering = entering + pick(before(chip ^ (mask >> 1), chip), array)
            cluster = cluster + array
    low = chip & 3
    sums = []
    for j in range(4):
        value = entering
        for i in range(4):
            if i != j:
                value = value + pick(before(low ^ i, low ^ j), parts[i])
        sums.append(value)
    rounded = [value.astype(BF16) for value in sums[1:]]
    arrived = [swap(rounded[j - 1], SCATTER[j - 1], count) for j in (1, 2, 3)]
    arrived, third = beside(arrived, works[2], rounded[0])
    entering = jnp.stack([sums[0], *(a.astype(F32) for a in arrived)])
    core = place & 1
    mine = entering + pick(before(core ^ 1, core), from_core)
    theirs = entering + pick(before(core, core ^ 1), own)
    return mine.astype(BF16), theirs.astype(BF16), (first, second, third)


def body(query_rows, key_rows, value_rows, grad_out):
    rows, width = query_rows.shape
    heads = width // HD
    half = heads // 2
    count = lax.axis_size("grp") * lax.axis_size("shard")
    place = lax.axis_index(AXES)
    key = slot_key(place, count).astype(jnp.int32).reshape(1)
    work = rows * width * HD
    scores = rows * width * rows
    block = (half, rows, HD)
    flat = (rows, width)
    dma = pltpu.SemaphoreType.DMA((2, half))
    buffer = pltpu.VMEM(block, BF16)

    def state(base, dtype, key):
        return call(
            functools.partial(state_kernel, base), [((half, HD, HD), dtype)], (key, key_rows, value_rows),
            work, in_hbm=(1, 2), scratch=(buffer, buffer, dma),
        )[0]

    def tied(tie):
        return lax.optimization_barrier((key, tie))[0]

    def local(tie):
        return call(
            local_kernel,
            [((heads, rows, HD), F32), ((heads, HD, rows), BF16), ((heads, rows, rows), BF16)],
            (tied(tie), query_rows, key_rows, value_rows), 6 * scores,
        )

    send = state(half, BF16, key)
    own = state(0, F32, tied(send))
    from_core = swap(send, 1, count).astype(F32)
    mine, theirs, (_, (mixed, turned, turned_scores), _) = scan_states(
        own, from_core, place, count, False, (None, local, None)
    )
    e_other = swap(theirs, 1, count)

    def norm(base, key, e, dtype):
        return call(
            functools.partial(norm_kernel, base),
            [(block, BF16), (block, BF16), ((half, HD, HD), dtype)],
            (key, query_rows, grad_out, turned, mixed, e), 2 * work,
        )

    att_mine, gm_mine, send = norm(0, key, mine, BF16)
    from_core = swap(send, 1, count).astype(F32)
    att_other, gm_other, own = norm(half, tied(send), e_other, F32)

    def grads(base, key, att, gm, e, outs):
        n = 8
        return call(
            functools.partial(grads_kernel, base),
            [(flat, BF16), (flat, BF16), (block, F32), (block, F32)],
            (key, query_rows, key_rows, value_rows, att, gm, e, turned_scores, *outs),
            4 * scores + work, out_hbm=2, in_hbm=(n, n + 1), scratch=(buffer, dma),
            aliases={n: 0, n + 1: 1} if outs else None,
        )

    def grads_mine(tie):
        return grads(0, tied(tie), att_mine, gm_mine, mine, ())

    made = []

    def grads_first(tie):
        made.append(grads_mine(tie))
        return made[0]

    def grads_second(tie):
        return grads(half, tied(tie), att_other, gm_other, e_other, made[0][:2])

    l_other, theirs, ((_, _, kl_mine, vl_mine), (attended, grad_query, kl_other, vl_other), _) = scan_states(
        own, from_core, place, count, True, (grads_first, grads_second, None)
    )
    l_mine = swap(theirs, 1, count)

    def last(base, key, kl, vl, later, outs):
        n = 6
        return call(
            functools.partial(last_kernel, base),
            [(flat, BF16), (flat, BF16)],
            (key, key_rows, value_rows, kl, vl, later, *outs),
            2 * work, out_hbm=2, in_hbm=(n, n + 1), scratch=(buffer, buffer, dma),
            aliases={n: 0, n + 1: 1} if outs else None,
        )

    outs = last(half, key, kl_other, vl_other, l_other, ())
    grad_key, grad_value = last(0, key, kl_mine, vl_mine, l_mine, outs)
    return attended, grad_query, grad_key, grad_value


def solution(mesh):
    spec = P(AXES, None)
    return jax.shard_map(
        body, mesh=mesh, in_specs=(spec,) * 4, out_specs=(spec,) * 4, check_vma=False
    )
```

```python
import functools
import math

import jax
import jax.numpy as jnp
from jax import lax
from jax.experimental import pallas as pl
from jax.experimental.pallas import tpu as pltpu
from jax.sharding import PartitionSpec as P

HD = 128
AXES = ("grp", "shard")
F32 = jnp.float32
BF16 = jnp.bfloat16


def dot(a, b, a_dim, b_dim):
    return lax.dot_general(a, b, (((a_dim,), (b_dim,)), ((), ())), preferred_element_type=F32)


def columns(slot, key):
    return pl.ds(pl.multiple_of((slot ^ key) * HD, HD), HD)


def triangle(rows, keep_lower):
    at_row = lax.broadcasted_iota(jnp.int32, (rows, rows), 0)
    at_col = lax.broadcasted_iota(jnp.int32, (rows, rows), 1)
    return at_row >= at_col if keep_lower else at_row <= at_col


def call(kernel, outs, args, flops, out_hbm=0, in_hbm=(), scratch=(), aliases=None):
    smem = pl.BlockSpec(memory_space=pltpu.SMEM)
    vmem = pl.BlockSpec(memory_space=pltpu.VMEM)
    hbm = pl.BlockSpec(memory_space=pltpu.HBM)
    shapes = [
        jax.ShapeDtypeStruct(shape, dtype) if i < out_hbm else pltpu.VMEM(shape, dtype)
        for i, (shape, dtype) in enumerate(outs)
    ]
    size = sum(math.prod(a.shape) * jnp.dtype(a.dtype).itemsize for a in (*args, *shapes))
    args = [pltpu.with_memory_space_constraint(a, pltpu.HBM) if i in in_hbm else a for i, a in enumerate(args)]
    specs = [smem if a.dtype == jnp.int32 else hbm if i in in_hbm else vmem for i, a in enumerate(args)]
    return pl.pallas_call(
        kernel,
        out_shape=shapes,
        in_specs=specs,
        out_specs=[hbm if i < out_hbm else vmem for i in range(len(shapes))],
        scratch_shapes=list(scratch),
        input_output_aliases=aliases or {},
        compiler_params=pltpu.CompilerParams(vmem_limit_bytes=12 * 1024 * 1024),
        cost_estimate=pl.CostEstimate(flops=flops, bytes_accessed=size, transcendentals=0),
    )(*args)


def send_kernel(key_ref, k_hbm, v_hbm, out_ref, k_ref, v_ref, sems):
    key = key_ref[0]
    half = out_ref.shape[0]
    copies = []
    for part in range(2):
        start = pl.multiple_of(((1 - part) * half ^ (key & half)) * HD, half * HD)
        cols = pl.ds(start, half * HD)
        for at, (hbm, ref) in enumerate(((k_hbm, k_ref), (v_hbm, v_ref))):
            copies.append(pltpu.make_async_copy(hbm.at[:, cols], ref.at[:, cols], sems.at[part, at]))
            copies[-1].start()
    for copy in copies[:2]:
        copy.wait()
    for j in range(half):
        cols = columns(half + j, key)
        out_ref[j] = dot(k_ref[:, cols], v_ref[:, cols], 0, 0).astype(BF16)
    for copy in copies[2:]:
        copy.wait()


def own_kernel(key_ref, k_ref, v_ref, out_ref):
    key = key_ref[0]
    for j in range(out_ref.shape[0]):
        cols = columns(j, key)
        out_ref[j] = dot(k_ref[:, cols], v_ref[:, cols], 0, 0).astype(BF16)


def local_kernel(key_ref, q_ref, k_ref, v_ref, mixed_ref, turned_ref):
    key = key_ref[0]
    rows = q_ref.shape[0]
    low = triangle(rows, True)
    for s in range(mixed_ref.shape[0]):
        cols = columns(s, key)
        q = q_ref[:, cols]
        k = k_ref[:, cols]
        scores = jnp.where(low, dot(q, k, 1, 1), 0.0).astype(BF16)
        mixed_ref[s] = dot(scores, v_ref[:, cols], 1, 0)
        turned_ref[s] = q.T


def norm_kernel(base, key_ref, q_ref, g_ref, turned_ref, mixed_ref, e_ref, att_ref, gm_ref, state_ref):
    key = key_ref[0]
    for j in range(e_ref.shape[0]):
        cols = columns(base + j, key)
        mixed = mixed_ref[base + j] + dot(q_ref[:, cols], e_ref[j], 1, 0)
        inv_rms = lax.rsqrt(jnp.mean(mixed * mixed, axis=-1, keepdims=True) + 1.0)
        normed = mixed * inv_rms
        att_ref[j] = normed.astype(BF16)
        g = g_ref[:, cols].astype(F32)
        gm = ((g - normed * jnp.mean(g * normed, axis=-1, keepdims=True)) * inv_rms).astype(BF16)
        gm_ref[j] = gm
        state_ref[j] = dot(turned_ref[base + j], gm, 1, 0).astype(state_ref.dtype)


def grads_kernel(base, key_ref, q_ref, k_ref, v_ref, att_ref, gm_ref, e_ref, *refs):
    att_hbm, gq_hbm, kl_ref, vl_ref, gq_buf, sems = refs[-6:]
    key = key_ref[0]
    rows = q_ref.shape[0]
    low = triangle(rows, True)
    high = triangle(rows, False)
    copies = []
    for j in range(e_ref.shape[0]):
        cols = columns(base + j, key)
        copies.append(pltpu.make_async_copy(att_ref.at[j], att_hbm.at[:, cols], sems.at[0, j]))
        copies[-1].start()
        q = q_ref[:, cols]
        k = k_ref[:, cols]
        v = v_ref[:, cols]
        gm = gm_ref[j]
        gs = jnp.where(low, dot(gm, v, 1, 1), 0.0).astype(BF16)
        gq_buf[j] = (dot(gs, k, 1, 0) + dot(gm, e_ref[j], 1, 1)).astype(BF16)
        copies.append(pltpu.make_async_copy(gq_buf.at[j], gq_hbm.at[:, cols], sems.at[1, j]))
        copies[-1].start()
        gs_turned = jnp.where(high, dot(v, gm, 1, 1), 0.0).astype(BF16)
        kl_ref[j] = dot(gs_turned, q, 1, 0).astype(BF16)
        scores = jnp.where(high, dot(k, q, 1, 1), 0.0).astype(BF16)
        vl_ref[j] = dot(scores, gm, 1, 0).astype(BF16)
    for copy in copies:
        copy.wait()


def last_kernel(base, key_ref, k_ref, v_ref, kl_ref, vl_ref, l_ref, *refs):
    gk_hbm, gv_hbm, gk_buf, gv_buf, sems = refs[-5:]
    key = key_ref[0]
    copies = []
    for j in range(l_ref.shape[0]):
        cols = columns(base + j, key)
        later = l_ref[j]
        gk_buf[j] = (kl_ref[j] + dot(v_ref[:, cols], later, 1, 1)).astype(BF16)
        copies.append(pltpu.make_async_copy(gk_buf.at[j], gk_hbm.at[:, cols], sems.at[0, j]))
        copies[-1].start()
        gv_buf[j] = (vl_ref[j] + dot(k_ref[:, cols], later, 1, 0)).astype(BF16)
        copies.append(pltpu.make_async_copy(gv_buf.at[j], gv_hbm.at[:, cols], sems.at[1, j]))
        copies[-1].start()
    for copy in copies:
        copy.wait()


def swap(array, mask, count):
    return lax.ppermute(array, AXES, [(i, i ^ mask) for i in range(count)])


def exchange_levels(count):
    bits = count.bit_length() - 1
    levels = []
    bit = 3
    while bit < bits:
        first = (1 << bit) | 1
        if bit + 1 < bits:
            second = 1 << (bit + 1)
            levels.append((first | second, second, first))
        else:
            levels.append((first,))
        bit += 2
    return levels


SCATTER = (3, 4, 7)


def slot_key(place, count):
    bits = count.bit_length() - 1
    half = (place ^ (place >> 1)) & 1
    for bit in range(3, bits, 2):
        half = half ^ ((place >> bit) & 1)
    return (half << 2) | ((place >> 1) & 3)


def beside(arrays, work, tie):
    if work is None:
        return arrays, None
    done = work(tie)
    return lax.optimization_barrier((arrays, done))


def scan_states(own, from_core, place, count, backward, works):
    def before(a, b):
        return (a > b) if backward else (a < b)

    def pick(condition, array):
        return jnp.where(condition, array, 0.0)

    chip = place >> 1
    own = own.astype(F32)
    total = own + from_core
    rounded = total.astype(BF16)
    arrived = [swap(rounded[j], SCATTER[j - 1], count) for j in (1, 2, 3)]
    arrived, first = beside(arrived, works[0], rounded)
    parts = [total[0], *(a.astype(F32) for a in arrived)]
    cluster = parts[0] + parts[1] + parts[2] + parts[3]
    entering = jnp.zeros_like(cluster)
    second = None
    for at, masks in enumerate(exchange_levels(count)):
        rounded = cluster.astype(BF16)
        arrived = [swap(rounded, mask, count) for mask in masks]
        if at == 0:
            arrived, second = beside(arrived, works[1], rounded)
        for mask, array in zip(masks, arrived):
            array = array.astype(F32)
            entering = entering + pick(before(chip ^ (mask >> 1), chip), array)
            cluster = cluster + array
    low = chip & 3
    sums = []
    for j in range(4):
        value = entering
        for i in range(4):
            if i != j:
                value = value + pick(before(low ^ i, low ^ j), parts[i])
        sums.append(value)
    rounded = [value.astype(BF16) for value in sums[1:]]
    arrived = [swap(rounded[j - 1], SCATTER[j - 1], count) for j in (1, 2, 3)]
    arrived, third = beside(arrived, works[2], rounded[0])
    entering = jnp.stack([sums[0], *(a.astype(F32) for a in arrived)])
    core = place & 1
    mine = entering + pick(before(core ^ 1, core), from_core)
    theirs = entering + pick(before(core, core ^ 1), own)
    return mine.astype(BF16), theirs.astype(BF16), (first, second, third)


def body(query_rows, key_rows, value_rows, grad_out):
    rows, width = query_rows.shape
    heads = width // HD
    half = heads // 2
    count = lax.axis_size("grp") * lax.axis_size("shard")
    place = lax.axis_index(AXES)
    key = slot_key(place, count).astype(jnp.int32).reshape(1)
    work = rows * width * HD
    scores = rows * width * rows
    block = (half, rows, HD)
    flat = (rows, width)
    dma = pltpu.SemaphoreType.DMA((2, half))
    buffer = pltpu.VMEM(block, BF16)

    def tied(tie):
        return lax.optimization_barrier((key, tie))[0]

    def local(tie):
        return call(
            local_kernel,
            [((heads, rows, HD), F32), ((heads, HD, rows), BF16)],
            (tied(tie), query_rows, keys, values), 4 * scores,
        )

    send, keys, values = call(
        send_kernel, [((half, HD, HD), BF16), (flat, BF16), (flat, BF16)], (key, key_rows, value_rows),
        work, in_hbm=(1, 2), scratch=(pltpu.SemaphoreType.DMA((2, 2)),),
    )
    (own,) = call(own_kernel, [((half, HD, HD), BF16)], (tied(send), keys, values), work)
    from_core = swap(send, 1, count).astype(F32)
    mine, theirs, (_, (mixed, turned), _) = scan_states(
        own, from_core, place, count, False, (None, local, None)
    )
    e_other = swap(theirs, 1, count)

    def norm(base, key, e, dtype):
        return call(
            functools.partial(norm_kernel, base),
            [(block, BF16), (block, BF16), ((half, HD, HD), dtype)],
            (key, query_rows, grad_out, turned, mixed, e), 2 * work,
        )

    att_mine, gm_mine, send = norm(0, key, mine, BF16)
    from_core = swap(send, 1, count).astype(F32)
    att_other, gm_other, own = norm(half, tied(send), e_other, BF16)

    def grads(base, key, att, gm, e, outs):
        n = 7
        return call(
            functools.partial(grads_kernel, base),
            [(flat, BF16), (flat, BF16), (block, BF16), (block, BF16)],
            (key, query_rows, keys, values, att, gm, e, *outs),
            4 * scores + work, out_hbm=2, in_hbm=(n, n + 1), scratch=(buffer, dma),
            aliases={n: 0, n + 1: 1} if outs else None,
        )

    def grads_mine(tie):
        return grads(0, tied(tie), att_mine, gm_mine, mine, ())

    made = []

    def grads_first(tie):
        made.append(grads_mine(tie))
        return made[0]

    def grads_second(tie):
        return grads(half, tied(tie), att_other, gm_other, e_other, made[0][:2])

    l_other, theirs, ((_, _, kl_mine, vl_mine), (attended, grad_query, kl_other, vl_other), _) = scan_states(
        own, from_core, place, count, True, (grads_first, grads_second, None)
    )
    l_mine = swap(theirs, 1, count)

    def last(base, key, kl, vl, later, outs):
        n = 6
        return call(
            functools.partial(last_kernel, base),
            [(flat, BF16), (flat, BF16)],
            (key, keys, values, kl, vl, later, *outs),
            2 * work, out_hbm=2, in_hbm=(n, n + 1), scratch=(buffer, buffer, dma),
            aliases={n: 0, n + 1: 1} if outs else None,
        )

    outs = last(half, key, kl_other, vl_other, l_other, ())
    grad_key, grad_value = last(0, key, kl_mine, vl_mine, l_mine, outs)
    return attended, grad_query, grad_key, grad_value


def solution(mesh):
    spec = P(AXES, None)
    return jax.shard_map(
        body, mesh=mesh, in_specs=(spec,) * 4, out_specs=(spec,) * 4, check_vma=False
    )
```

```python
import functools
import math

import jax
import jax.numpy as jnp
from jax import lax
from jax.experimental import pallas as pl
from jax.experimental.pallas import tpu as pltpu
from jax.sharding import PartitionSpec as P

HD = 128
COST = 3
AXES = ("grp", "shard")
F32 = jnp.float32
BF16 = jnp.bfloat16


def dot(a, b, a_dim, b_dim):
    return lax.dot_general(a, b, (((a_dim,), (b_dim,)), ((), ())), preferred_element_type=F32)


def columns(slot, key):
    return pl.ds(pl.multiple_of((slot ^ key) * HD, HD), HD)


def triangle(rows, keep_lower):
    at_row = lax.broadcasted_iota(jnp.int32, (rows, rows), 0)
    at_col = lax.broadcasted_iota(jnp.int32, (rows, rows), 1)
    return at_row >= at_col if keep_lower else at_row <= at_col


def call(kernel, outs, args, flops, out_hbm=0, in_hbm=(), scratch=(), aliases=None):
    smem = pl.BlockSpec(memory_space=pltpu.SMEM)
    vmem = pl.BlockSpec(memory_space=pltpu.VMEM)
    hbm = pl.BlockSpec(memory_space=pltpu.HBM)
    shapes = [
        jax.ShapeDtypeStruct(shape, dtype) if i < out_hbm else pltpu.VMEM(shape, dtype)
        for i, (shape, dtype) in enumerate(outs)
    ]
    size = sum(math.prod(a.shape) * jnp.dtype(a.dtype).itemsize for a in (*args, *shapes))
    args = [pltpu.with_memory_space_constraint(a, pltpu.HBM) if i in in_hbm else a for i, a in enumerate(args)]
    specs = [smem if a.dtype == jnp.int32 else hbm if i in in_hbm else vmem for i, a in enumerate(args)]
    return pl.pallas_call(
        kernel,
        out_shape=shapes,
        in_specs=specs,
        out_specs=[hbm if i < out_hbm else vmem for i in range(len(shapes))],
        scratch_shapes=list(scratch),
        input_output_aliases=aliases or {},
        compiler_params=pltpu.CompilerParams(vmem_limit_bytes=12 * 1024 * 1024),
        cost_estimate=pl.CostEstimate(flops=int(flops * COST), bytes_accessed=int(size * COST), transcendentals=0),
    )(*args)


def send_kernel(key_ref, k_hbm, v_hbm, out_ref, theirs_ref, mine_ref, sems):
    key = key_ref[0]
    half = out_ref.shape[0]
    copies = []
    for part, ref in enumerate((theirs_ref, mine_ref)):
        for at, hbm in enumerate((k_hbm, v_hbm)):
            copies.append(pltpu.make_async_copy(hbm.at[:, half_of(key, half, part)], ref.at[at], sems.at[part, at]))
            copies[-1].start()
    for copy in copies[:2]:
        copy.wait()
    for j in range(half):
        cols = half_columns(j, key, half)
        out_ref[j] = dot(theirs_ref[0, :, cols], theirs_ref[1, :, cols], 0, 0).astype(BF16)
    for copy in copies[2:]:
        copy.wait()


def own_kernel(key_ref, kv_ref, out_ref):
    key = key_ref[0]
    half = out_ref.shape[0]
    for j in range(half):
        cols = half_columns(j, key, half)
        out_ref[j] = dot(kv_ref[0, :, cols], kv_ref[1, :, cols], 0, 0).astype(BF16)


def fetch_kernel(half, key_ref, q_hbm, g_hbm, theirs_ref, mine_ref, sems):
    key = key_ref[0]
    copies = []
    for part, ref in enumerate((theirs_ref, mine_ref)):
        for at, hbm in enumerate((q_hbm, g_hbm)):
            copies.append(pltpu.make_async_copy(hbm.at[:, half_of(key, half, part)], ref.at[at], sems.at[part, at]))
            copies[-1].start()
    for copy in copies:
        copy.wait()


def half_of(key, half, mine):
    first = key & half
    if not mine:
        first = half ^ first
    return pl.ds(pl.multiple_of(first * HD, half * HD), half * HD)


def half_columns(slot, key, half):
    return pl.ds(pl.multiple_of(((slot ^ key) & (half - 1)) * HD, HD), HD)


def local_kernel(key_ref, kv_ref, qg_ref, their_kv_ref, their_qg_ref, mixed_ref):
    key = key_ref[0]
    half = mixed_ref.shape[1]
    low = triangle(mixed_ref.shape[2], True)
    for j in range(half):
        cols = half_columns(j, key, half)
        for at, (kv, qg) in enumerate(((kv_ref, qg_ref), (their_kv_ref, their_qg_ref))):
            scores = jnp.where(low, dot(qg[0, :, cols], kv[0, :, cols], 1, 1), 0.0).astype(BF16)
            mixed_ref[at, j] = dot(scores, kv[1, :, cols], 1, 0)


def norm_kernel(base, key_ref, qg_ref, their_qg_ref, mixed_ref, mine_ref, theirs_ref, att_ref, gm_ref, state_ref, pair_ref, their_state_ref):
    key = key_ref[0]
    half = mixed_ref.shape[1]
    for j in range(mine_ref.shape[0]):
        cols = half_columns(base + j, key, half)
        for at, (qg, e) in enumerate(((qg_ref, mine_ref), (their_qg_ref, theirs_ref))):
            q = qg[0, :, cols]
            mixed = mixed_ref[at, base + j] + dot(q, e[j], 1, 0)
            inv_rms = lax.rsqrt(jnp.mean(mixed * mixed, axis=-1, keepdims=True) + 1.0)
            normed = mixed * inv_rms
            g = qg[1, :, cols].astype(F32)
            gm = ((g - normed * jnp.mean(g * normed, axis=-1, keepdims=True)) * inv_rms).astype(BF16)
            state = dot(q, gm, 0, 0).astype(BF16)
            if at:
                pair_ref[0, j] = normed.astype(BF16)
                pair_ref[1, j] = gm
                their_state_ref[j] = state
            else:
                att_ref[j] = normed.astype(BF16)
                gm_ref[j] = gm
                state_ref[j] = state


def grads_kernel(base, pieces, key_ref, q_ref, k_ref, v_ref, *refs):
    att_refs, gm_refs, e_refs = (refs[i * pieces : (i + 1) * pieces] for i in range(3))
    att_hbm, gq_hbm, kl_ref, vl_ref, gq_buf, sems = refs[-6:]
    key = key_ref[0]
    rows = q_ref.shape[0]
    low = triangle(rows, True)
    high = triangle(rows, False)
    copies = []
    for j in range(gq_buf.shape[0]):
        piece, i = divmod(j, gq_buf.shape[0] // pieces)
        cols = columns(base + j, key)
        copies.append(pltpu.make_async_copy(att_refs[piece].at[i], att_hbm.at[:, cols], sems.at[0, j]))
        copies[-1].start()
        q = q_ref[:, cols]
        k = k_ref[:, cols]
        v = v_ref[:, cols]
        gm = gm_refs[piece][i]
        gs = jnp.where(low, dot(gm, v, 1, 1), 0.0).astype(BF16)
        gq_buf[j] = (dot(gs, k, 1, 0) + dot(gm, e_refs[piece][i], 1, 1)).astype(BF16)
        copies.append(pltpu.make_async_copy(gq_buf.at[j], gq_hbm.at[:, cols], sems.at[1, j]))
        copies[-1].start()
        gs_turned = jnp.where(high, dot(v, gm, 1, 1), 0.0).astype(BF16)
        kl_ref[j] = dot(gs_turned, q, 1, 0).astype(BF16)
        scores = jnp.where(high, dot(k, q, 1, 1), 0.0).astype(BF16)
        vl_ref[j] = dot(scores, gm, 1, 0).astype(BF16)
    for copy in copies:
        copy.wait()


def last_kernel(base, key_ref, k_ref, v_ref, kl_ref, vl_ref, l_ref, *refs):
    gk_hbm, gv_hbm, gk_buf, gv_buf, sems = refs[-5:]
    key = key_ref[0]
    copies = []
    for j in range(l_ref.shape[0]):
        cols = columns(base + j, key)
        later = l_ref[j]
        gk_buf[j] = (kl_ref[j] + dot(v_ref[:, cols], later, 1, 1)).astype(BF16)
        copies.append(pltpu.make_async_copy(gk_buf.at[j], gk_hbm.at[:, cols], sems.at[0, j]))
        copies[-1].start()
        gv_buf[j] = (vl_ref[j] + dot(k_ref[:, cols], later, 1, 0)).astype(BF16)
        copies.append(pltpu.make_async_copy(gv_buf.at[j], gv_hbm.at[:, cols], sems.at[1, j]))
        copies[-1].start()
    for copy in copies:
        copy.wait()


def swap(array, mask, count):
    return lax.ppermute(array, AXES, [(i, i ^ mask) for i in range(count)])


def exchange_levels(count):
    bits = count.bit_length() - 1
    levels = []
    bit = 3
    while bit < bits:
        first = (1 << bit) | 1
        if bit + 1 < bits:
            second = 1 << (bit + 1)
            levels.append(((3 << bit), (1 << bit) | 1, (2 << bit) | 1))
        else:
            levels.append((first,))
        bit += 2
    return levels


ORDER = (1, 3, 2)
SCATTER = (3, 4, 7)


GROUPS = ((0, 1), (2, 3))


def slot_key(place, count):
    bits = count.bit_length() - 1
    half = (place ^ (place >> 1)) & 1
    for bit in range(3, bits, 2):
        half = half ^ ((place >> (bit + 0)) ^ (place >> (bit + 1))) & 1
    return (half << 2) | ((place >> 1) & 3)


def beside(arrays, work, tie):
    if work is None:
        return arrays, None
    done = work(tie)
    return lax.optimization_barrier((arrays, done))


def pick(condition, array):
    return jnp.where(condition, array, 0.0)


def tie_to(array, other):
    return lax.optimization_barrier((array, other))[0]


def merge(own, from_core, place, count, backward, works):
    def before(a, b):
        return (a > b) if backward else (a < b)

    chip = place >> 1
    total = [a.astype(F32) + b.astype(F32) for a, b in zip(own, from_core)]
    rounded = [t.astype(BF16) for t in total]
    arrived = {j: swap(rounded[j], SCATTER[j - 1], count) for j in ORDER}
    arrived = [arrived[j] for j in (1, 2, 3)]
    if works[0] is not None and works[0][1]:
        first = works[0][0](arrived[ORDER[0] - 1])
    else:
        arrived, first = beside(arrived, works[0] and works[0][0], rounded[ORDER[0]])
    parts = [total[0], *(a.astype(F32) for a in arrived)]
    cluster = parts[0] + parts[1] + parts[2] + parts[3]
    entering = jnp.zeros_like(cluster)
    second = None
    for at, masks in enumerate(exchange_levels(count)):
        rounded = cluster.astype(BF16)
        arrived = [swap(rounded, mask, count) for mask in masks]
        if at == 0:
            arrived, second = beside(arrived, works[1], rounded)
        for mask, array in zip(masks, arrived):
            array = array.astype(F32)
            entering = entering + pick(before(chip ^ (mask >> 1), chip), array)
            cluster = cluster + array
    low = chip & 3
    sums = []
    for j in range(4):
        value = entering
        for i in range(4):
            if i != j:
                value = value + pick(before(low ^ i, low ^ j), parts[i])
        sums.append(value)
    rounded = [value.astype(BF16) for value in sums]
    arrived = {j: swap(rounded[j], SCATTER[j - 1], count) for j in ORDER}
    arrived = [arrived[j] for j in (1, 2, 3)]
    arrived, third = beside(arrived, works[2], rounded[1])
    return [sums[0], *arrived], (first, second, third)


def share(slots, entering, own, from_core, place, backward):
    first = (place & 1) == (1 if backward else 0)
    entering = jnp.stack([e.astype(F32) for e in entering])
    mine = entering + pick(~first, jnp.stack([from_core[j].astype(F32) for j in slots]))
    theirs = entering + pick(first, jnp.stack([own[j].astype(F32) for j in slots]))
    return mine.astype(BF16), theirs.astype(BF16)


def body(query_rows, key_rows, value_rows, grad_out):
    rows, width = query_rows.shape
    heads = width // HD
    half = heads // 2
    count = lax.axis_size("grp") * lax.axis_size("shard")
    place = lax.axis_index(AXES)
    key = slot_key(place, count).astype(jnp.int32).reshape(1)
    work = rows * width * HD
    scores = rows * width * rows
    block = (half, rows, HD)
    flat = (rows, width)
    dma = pltpu.SemaphoreType.DMA((2, half))
    buffer = pltpu.VMEM(block, BF16)

    def tied(tie):
        return lax.optimization_barrier((key, tie))[0]

    wide = (2, rows, width // 2)
    pairs = pltpu.SemaphoreType.DMA((2, 2))
    send, kv_send, kv_own = call(
        send_kernel, [((half, HD, HD), BF16), (wide, BF16), (wide, BF16)], (key, key_rows, value_rows),
        work, in_hbm=(1, 2), scratch=(pairs,),
    )
    (own,) = call(own_kernel, [((half, HD, HD), BF16)], (tied(send), kv_own), work)
    from_core = swap(send, 1, count)
    brought = []

    def fetch(tie):
        brought.extend(call(
            functools.partial(fetch_kernel, half), [(wide, BF16), (wide, BF16)],
            (tied(tie), query_rows, grad_out), 0, in_hbm=(1, 2), scratch=(pairs,),
        ))
        return brought

    def local(tie):
        qg_send, qg_own = brought
        kv = swap(tie_to(kv_send, tie), 1, count)
        qg = swap(tie_to(qg_send, tie), 1, count)
        brought.append(qg)
        return call(
            local_kernel, [((2, half, rows, HD), F32)], (tied(tie), kv_own, qg_own, kv, qg), 4 * scores,
        )[0]

    entering, ((_, qg_own), mixed, _) = merge(own, from_core, place, count, False, ((fetch, False), local, None))

    qg = brought[2]

    def norm(slot, mine, theirs):
        n = mine.shape[0]
        rows_of = (n, rows, HD)
        states = (n, HD, HD)
        return call(
            functools.partial(norm_kernel, slot),
            [(rows_of, BF16), (rows_of, BF16), (states, BF16), ((2, *rows_of), BF16), (states, BF16)],
            (key, qg_own, qg, mixed, mine, theirs), n * work // 2,
        )

    inner, outer = [], []
    own_back, core_back = [], []
    for at, group in enumerate(GROUPS):
        come = [entering[j] for j in group]
        if at:
            come = tie_to(come, state)
        mine, theirs = share(group, come, own, from_core, place, False)
        att, gm, state, pair, their_state = norm(group[0], mine, theirs)
        inner.append((att, gm, mine))
        outer.append((pair, theirs))
        own_back += [state[i] for i in range(len(group))]
        core_back += [their_state[i] for i in range(len(group))]

    late_q, late_k, late_v = tie_to((query_rows, key_rows, value_rows), mixed)

    def grads(base, key, parts, outs):
        att, gm, e = ([p[i] for p in parts] for i in range(3))
        n = 4 + 3 * len(parts)
        return call(
            functools.partial(grads_kernel, base, len(parts)),
            [(flat, BF16), (flat, BF16), (block, BF16), (block, BF16)],
            (key, late_q, late_k, late_v, *att, *gm, *e, *outs),
            4 * scores + work, out_hbm=2, in_hbm=(n, n + 1), scratch=(buffer, dma),
            aliases={n: 0, n + 1: 1} if outs else None,
        )

    made = []

    def grads_first(tie):
        made.append(grads(0, tied(tie), inner, ()))
        return made[0]

    def grads_second(tie):
        parts = []
        for pair, theirs in outer:
            pair = swap(pair, 1, count)
            parts.append((pair[0], pair[1], swap(theirs, 1, count)))
        return grads(half, tied(tie), parts, made[0][:2])

    entering, ((_, _, kl_mine, vl_mine), (attended, grad_query, kl_other, vl_other), _) = merge(
        own_back, core_back, place, count, True, ((grads_first, False), grads_second, None)
    )
    l_mine, theirs = share(range(half), entering, own_back, core_back, place, True)
    l_other = swap(theirs, 1, count)

    def last(base, key, kl, vl, later, outs):
        n = 6
        return call(
            functools.partial(last_kernel, base),
            [(flat, BF16), (flat, BF16)],
            (key, late_k, late_v, kl, vl, later, *outs),
            2 * work, out_hbm=2, in_hbm=(n, n + 1), scratch=(buffer, buffer, dma),
            aliases={n: 0, n + 1: 1} if outs else None,
        )

    outs = last(0, key, kl_mine, vl_mine, l_mine, ())
    grad_key, grad_value = last(half, key, kl_other, vl_other, l_other, outs)
    return attended, grad_query, grad_key, grad_value


def solution(mesh):
    spec = P(AXES, None)
    return jax.shard_map(
        body, mesh=mesh, in_specs=(spec,) * 4, out_specs=(spec,) * 4, check_vma=False
    )
```

```python
import functools
import itertools
import math

import jax
import jax.numpy as jnp
from jax import lax
from jax.experimental import pallas as pl
from jax.experimental.pallas import tpu as pltpu
from jax.sharding import PartitionSpec as P

HD = 128
COST = 3
AXES = ("grp", "shard")
F32 = jnp.float32
BF16 = jnp.bfloat16


def dot(a, b, a_dim, b_dim):
    return lax.dot_general(a, b, (((a_dim,), (b_dim,)), ((), ())), preferred_element_type=F32)


def columns(slot, key):
    return pl.ds(pl.multiple_of((slot ^ key) * HD, HD), HD)


def triangle(rows, keep_lower):
    at_row = lax.broadcasted_iota(jnp.int32, (rows, rows), 0)
    at_col = lax.broadcasted_iota(jnp.int32, (rows, rows), 1)
    return at_row >= at_col if keep_lower else at_row <= at_col


def call(kernel, outs, args, flops, out_hbm=0, in_hbm=(), scratch=(), aliases=None):
    smem = pl.BlockSpec(memory_space=pltpu.SMEM)
    vmem = pl.BlockSpec(memory_space=pltpu.VMEM)
    hbm = pl.BlockSpec(memory_space=pltpu.HBM)
    shapes = [
        jax.ShapeDtypeStruct(shape, dtype) if i < out_hbm else pltpu.VMEM(shape, dtype)
        for i, (shape, dtype) in enumerate(outs)
    ]
    size = sum(math.prod(a.shape) * jnp.dtype(a.dtype).itemsize for a in (*args, *shapes))
    args = [pltpu.with_memory_space_constraint(a, pltpu.HBM) if i in in_hbm else a for i, a in enumerate(args)]
    specs = [smem if a.dtype == jnp.int32 else hbm if i in in_hbm else vmem for i, a in enumerate(args)]
    return pl.pallas_call(
        kernel,
        out_shape=shapes,
        in_specs=specs,
        out_specs=[hbm if i < out_hbm else vmem for i in range(len(shapes))],
        scratch_shapes=list(scratch),
        input_output_aliases=aliases or {},
        compiler_params=pltpu.CompilerParams(vmem_limit_bytes=12 * 1024 * 1024),
        cost_estimate=pl.CostEstimate(flops=int(flops * COST), bytes_accessed=int(size * COST), transcendentals=0),
    )(*args)


def send_kernel(key_ref, k_hbm, v_hbm, out_ref, theirs_ref, mine_ref, sems):
    key = key_ref[0]
    half = out_ref.shape[0]
    copies = []
    for part, ref in enumerate((theirs_ref, mine_ref)):
        for at, hbm in enumerate((k_hbm, v_hbm)):
            copies.append(pltpu.make_async_copy(hbm.at[:, half_of(key, half, part)], ref.at[at], sems.at[part, at]))
            copies[-1].start()
    for copy in copies[:2]:
        copy.wait()
    for j in range(half):
        cols = half_columns(j, key, half)
        out_ref[j] = dot(theirs_ref[0, :, cols], theirs_ref[1, :, cols], 0, 0).astype(BF16)
    for copy in copies[2:]:
        copy.wait()


def own_kernel(key_ref, kv_ref, out_ref):
    key = key_ref[0]
    half = out_ref.shape[0]
    for j in range(half):
        cols = half_columns(j, key, half)
        out_ref[j] = dot(kv_ref[0, :, cols], kv_ref[1, :, cols], 0, 0).astype(BF16)


def fetch_kernel(half, key_ref, q_hbm, g_hbm, theirs_ref, mine_ref, sems):
    key = key_ref[0]
    copies = []
    for part, ref in enumerate((theirs_ref, mine_ref)):
        for at, hbm in enumerate((q_hbm, g_hbm)):
            copies.append(pltpu.make_async_copy(hbm.at[:, half_of(key, half, part)], ref.at[at], sems.at[part, at]))
            copies[-1].start()
    for copy in copies:
        copy.wait()


def half_of(key, half, mine):
    first = key & half
    if not mine:
        first = half ^ first
    return pl.ds(pl.multiple_of(first * HD, half * HD), half * HD)


def half_columns(slot, key, half):
    return pl.ds(pl.multiple_of(((slot ^ key) & (half - 1)) * HD, HD), HD)


def local_kernel(key_ref, kv_ref, qg_ref, their_kv_ref, their_qg_ref, mixed_ref):
    key = key_ref[0]
    half = mixed_ref.shape[1]
    low = triangle(mixed_ref.shape[2], True)
    for j in range(half):
        cols = half_columns(j, key, half)
        for at, (kv, qg) in enumerate(((kv_ref, qg_ref), (their_kv_ref, their_qg_ref))):
            scores = jnp.where(low, dot(qg[0, :, cols], kv[0, :, cols], 1, 1), 0.0).astype(BF16)
            mixed_ref[at, j] = dot(scores, kv[1, :, cols], 1, 0)


def norm_kernel(base, key_ref, qg_ref, their_qg_ref, mixed_ref, mine_ref, theirs_ref, att_ref, gm_ref, state_ref, pack_ref, their_state_ref):
    key = key_ref[0]
    half, rows = mixed_ref.shape[1:3]
    for j in range(mine_ref.shape[0]):
        cols = half_columns(base + j, key, half)
        for at, (qg, e) in enumerate(((qg_ref, mine_ref), (their_qg_ref, theirs_ref))):
            q = qg[0, :, cols]
            mixed = mixed_ref[at, base + j] + dot(q, e[j], 1, 0)
            inv_rms = lax.rsqrt(jnp.mean(mixed * mixed, axis=-1, keepdims=True) + 1.0)
            normed = mixed * inv_rms
            g = qg[1, :, cols].astype(F32)
            gm = ((g - normed * jnp.mean(g * normed, axis=-1, keepdims=True)) * inv_rms).astype(BF16)
            state = dot(q, gm, 0, 0).astype(BF16)
            if at:
                pack_ref[j, :rows] = normed.astype(BF16)
                pack_ref[j, rows : 2 * rows] = gm
                pack_ref[j, 2 * rows :] = e[j]
                their_state_ref[j] = state
            else:
                att_ref[j] = normed.astype(BF16)
                gm_ref[j] = gm
                state_ref[j] = state


def grads_kernel(base, per_group, key_ref, q_ref, k_ref, v_ref, *refs):
    att_hbm, gq_hbm, kl_ref, vl_ref, gq_buf, sems = refs[-6:]
    key = key_ref[0]
    rows = q_ref.shape[0]
    low = triangle(rows, True)
    high = triangle(rows, False)
    slots = []
    for at in range(0, per_group * len(GROUPS), per_group):
        group = refs[at : at + per_group]
        for i in range(group[0].shape[0]):
            if per_group == 1:
                slots.append([group[0].at[i, pl.ds(start, n)] for start, n in ((0, rows), (rows, rows), (2 * rows, HD))])
            else:
                slots.append([ref.at[i] for ref in group])
    copies = []
    for j, (att, gm_ref, e_ref) in enumerate(slots):
        cols = columns(base + j, key)
        copies.append(pltpu.make_async_copy(att, att_hbm.at[:, cols], sems.at[0, j]))
        copies[-1].start()
        q = q_ref[:, cols]
        k = k_ref[:, cols]
        v = v_ref[:, cols]
        gm = gm_ref[...]
        gs = jnp.where(low, dot(gm, v, 1, 1), 0.0).astype(BF16)
        gq_buf[j] = (dot(gs, k, 1, 0) + dot(gm, e_ref[...], 1, 1)).astype(BF16)
        copies.append(pltpu.make_async_copy(gq_buf.at[j], gq_hbm.at[:, cols], sems.at[1, j]))
        copies[-1].start()
        gs_turned = jnp.where(high, dot(v, gm, 1, 1), 0.0).astype(BF16)
        kl_ref[j] = dot(gs_turned, q, 1, 0).astype(BF16)
        scores = jnp.where(high, dot(k, q, 1, 1), 0.0).astype(BF16)
        vl_ref[j] = dot(scores, gm, 1, 0).astype(BF16)
    for copy in copies:
        copy.wait()


def last_kernel(base, key_ref, k_ref, v_ref, kl_ref, vl_ref, l_ref, *refs):
    gk_hbm, gv_hbm, gk_buf, gv_buf, sems = refs[-5:]
    key = key_ref[0]
    copies = []
    for j in range(l_ref.shape[0]):
        cols = columns(base + j, key)
        later = l_ref[j]
        gk_buf[j] = (kl_ref[j] + dot(v_ref[:, cols], later, 1, 1)).astype(BF16)
        copies.append(pltpu.make_async_copy(gk_buf.at[j], gk_hbm.at[:, cols], sems.at[0, j]))
        copies[-1].start()
        gv_buf[j] = (vl_ref[j] + dot(k_ref[:, cols], later, 1, 0)).astype(BF16)
        copies.append(pltpu.make_async_copy(gv_buf.at[j], gv_hbm.at[:, cols], sems.at[1, j]))
        copies[-1].start()
    for copy in copies:
        copy.wait()


def swap(array, mask, count):
    return lax.ppermute(array, AXES, [(i, i ^ mask) for i in range(count)])


def exchange_levels(count):
    bits = count.bit_length() - 1
    levels = []
    bit = 3
    while bit < bits:
        first = (1 << bit) | 1
        if bit + 1 < bits:
            second = 1 << (bit + 1)
            levels.append(((3 << bit), (1 << bit) | 1, (2 << bit) | 1))
        else:
            levels.append((first,))
        bit += 2
    return levels


ORDER = (1, 2, 3)
SCATTER = (3, 4, 7)


GROUPS = ((0, 1), (2, 3))


def slot_key(place, count):
    bits = count.bit_length() - 1
    half = (place ^ (place >> 1)) & 1
    for bit in range(3, bits, 2):
        half = half ^ ((place >> (bit + 0)) ^ (place >> (bit + 1))) & 1
    return (half << 2) | ((place >> 1) & 3)


def beside(arrays, work, tie):
    if work is None:
        return arrays, None
    done = work(tie)
    return lax.optimization_barrier((arrays, done))


def pick(condition, array):
    return jnp.where(condition, array, 0.0)


def tie_to(array, other):
    return lax.optimization_barrier((array, other))[0]


def merge(own, from_core, place, count, backward, works):
    def before(a, b):
        return (a > b) if backward else (a < b)

    chip = place >> 1
    total = [a.astype(F32) + b.astype(F32) for a, b in zip(own, from_core)]
    rounded = [t.astype(BF16) for t in total]
    arrived = {j: swap(rounded[j], SCATTER[j - 1], count) for j in ORDER}
    arrived = [arrived[j] for j in (1, 2, 3)]
    if works[0] is not None and works[0][1]:
        first = works[0][0](arrived[ORDER[0] - 1])
    else:
        arrived, first = beside(arrived, works[0] and works[0][0], rounded[ORDER[0]])
    parts = [total[0], *(a.astype(F32) for a in arrived)]
    cluster = parts[0] + parts[1] + parts[2] + parts[3]
    entering = jnp.zeros_like(cluster)
    second = None
    for at, masks in enumerate(exchange_levels(count)):
        rounded = cluster.astype(BF16)
        arrived = [swap(rounded, mask, count) for mask in masks]
        if at == 0:
            arrived, second = beside(arrived, works[1], rounded)
        for mask, array in zip(masks, arrived):
            array = array.astype(F32)
            entering = entering + pick(before(chip ^ (mask >> 1), chip), array)
            cluster = cluster + array
    low = chip & 3
    sums = []
    for j in range(4):
        value = entering
        for i in range(4):
            if i != j:
                value = value + pick(before(low ^ i, low ^ j), parts[i])
        sums.append(value)
    rounded = [value.astype(BF16) for value in sums]
    arrived = {j: swap(rounded[j], SCATTER[j - 1], count) for j in ORDER}
    arrived = [arrived[j] for j in (1, 2, 3)]
    arrived, third = beside(arrived, works[2], rounded[1])
    return [sums[0], *arrived], (first, second, third)


def share(slots, entering, own, from_core, place, backward):
    first = (place & 1) == (1 if backward else 0)
    entering = jnp.stack([e.astype(F32) for e in entering])
    mine = entering + pick(~first, jnp.stack([from_core[j].astype(F32) for j in slots]))
    theirs = entering + pick(first, jnp.stack([own[j].astype(F32) for j in slots]))
    return mine.astype(BF16), theirs.astype(BF16)


def body(query_rows, key_rows, value_rows, grad_out):
    rows, width = query_rows.shape
    heads = width // HD
    half = heads // 2
    count = lax.axis_size("grp") * lax.axis_size("shard")
    place = lax.axis_index(AXES)
    key = slot_key(place, count).astype(jnp.int32).reshape(1)
    work = rows * width * HD
    scores = rows * width * rows
    block = (half, rows, HD)
    flat = (rows, width)
    dma = pltpu.SemaphoreType.DMA((2, half))
    buffer = pltpu.VMEM(block, BF16)

    def tied(tie):
        return lax.optimization_barrier((key, tie))[0]

    wide = (2, rows, width // 2)
    pairs = pltpu.SemaphoreType.DMA((2, 2))
    send, kv_send, kv_own = call(
        send_kernel, [((half, HD, HD), BF16), (wide, BF16), (wide, BF16)], (key, key_rows, value_rows),
        work, in_hbm=(1, 2), scratch=(pairs,),
    )
    (own,) = call(own_kernel, [((half, HD, HD), BF16)], (tied(send), kv_own), work)
    from_core = swap(send, 1, count)
    brought = []

    def fetch(tie):
        brought.extend(call(
            functools.partial(fetch_kernel, half), [(wide, BF16), (wide, BF16)],
            (tied(tie), query_rows, grad_out), 0, in_hbm=(1, 2), scratch=(pairs,),
        ))
        return brought

    def local(tie):
        qg_send, qg_own = brought
        kv = swap(tie_to(kv_send, tie), 1, count)
        qg = swap(tie_to(qg_send, tie), 1, count)
        brought.append(qg)
        return call(
            local_kernel, [((2, half, rows, HD), F32)], (tied(tie), kv_own, qg_own, kv, qg), 4 * scores,
        )[0]

    entering, ((_, qg_own), mixed, _) = merge(own, from_core, place, count, False, ((fetch, False), local, None))

    qg = brought[2]

    def norm(slot, mine, theirs):
        n = mine.shape[0]
        rows_of = (n, rows, HD)
        states = (n, HD, HD)
        return call(
            functools.partial(norm_kernel, slot),
            [(rows_of, BF16), (rows_of, BF16), (states, BF16), ((n, 2 * rows + HD, HD), BF16), (states, BF16)],
            (key, qg_own, qg, mixed, mine, theirs), n * work // 2,
        )

    inner, outer = [], []
    own_back, core_back = [], []
    for at, group in enumerate(GROUPS):
        come = [entering[j] for j in group]
        if at:
            come = tie_to(come, state)
        mine, theirs = share(group, come, own, from_core, place, False)
        att, gm, state, pack, their_state = norm(group[0], mine, theirs)
        inner.append((att, gm, mine))
        outer.append(pack)
        own_back += [state[i] for i in range(len(group))]
        core_back += [their_state[i] for i in range(len(group))]

    late_q, late_k, late_v = tie_to((query_rows, key_rows, value_rows), mixed)

    def grads(base, key, parts, outs):
        per_group = len(parts[0])
        n = 4 + per_group * len(parts)
        return call(
            functools.partial(grads_kernel, base, per_group),
            [(flat, BF16), (flat, BF16), (block, BF16), (block, BF16)],
            (key, late_q, late_k, late_v, *itertools.chain(*parts), *outs),
            4 * scores + work, out_hbm=2, in_hbm=(n, n + 1), scratch=(buffer, dma),
            aliases={n: 0, n + 1: 1} if outs else None,
        )

    made = []

    def grads_first(tie):
        made.append(grads(0, tied(tie), inner, ()))
        return made[0]

    came = []

    def trade(tie):
        came.extend((swap(tie_to(pack, tie), 1, count),) for pack in outer)
        return ()

    def grads_second(tie):
        return grads(half, tied(tie), came, made[0][:2])

    entering, ((_, _, kl_mine, vl_mine), _, (attended, grad_query, kl_other, vl_other)) = merge(
        own_back, core_back, place, count, True, ((grads_first, False), trade, grads_second)
    )
    l_mine, theirs = share(range(half), entering, own_back, core_back, place, True)
    l_other = swap(theirs, 1, count)

    def last(base, key, kl, vl, later, outs):
        n = 6
        return call(
            functools.partial(last_kernel, base),
            [(flat, BF16), (flat, BF16)],
            (key, late_k, late_v, kl, vl, later, *outs),
            2 * work, out_hbm=2, in_hbm=(n, n + 1), scratch=(buffer, buffer, dma),
            aliases={n: 0, n + 1: 1} if outs else None,
        )

    outs = last(0, key, kl_mine, vl_mine, l_mine, ())
    grad_key, grad_value = last(half, key, kl_other, vl_other, l_other, outs)
    return attended, grad_query, grad_key, grad_value


def solution(mesh):
    spec = P(AXES, None)
    return jax.shard_map(
        body, mesh=mesh, in_specs=(spec,) * 4, out_specs=(spec,) * 4, check_vma=False
    )
```

```python
import functools
import itertools
import math

import jax
import jax.numpy as jnp
from jax import lax
from jax.experimental import pallas as pl
from jax.experimental.pallas import tpu as pltpu
from jax.sharding import PartitionSpec as P

HD = 128
COST = 3
AXES = ("grp", "shard")
F32 = jnp.float32
BF16 = jnp.bfloat16


def dot(a, b, a_dim, b_dim):
    return lax.dot_general(a, b, (((a_dim,), (b_dim,)), ((), ())), preferred_element_type=F32)


def columns(slot, key):
    return pl.ds(pl.multiple_of((slot ^ key) * HD, HD), HD)


def triangle(rows, keep_lower):
    at_row = lax.broadcasted_iota(jnp.int32, (rows, rows), 0)
    at_col = lax.broadcasted_iota(jnp.int32, (rows, rows), 1)
    return at_row >= at_col if keep_lower else at_row <= at_col


def call(kernel, outs, args, flops, out_hbm=0, in_hbm=(), scratch=(), aliases=None):
    smem = pl.BlockSpec(memory_space=pltpu.SMEM)
    vmem = pl.BlockSpec(memory_space=pltpu.VMEM)
    hbm = pl.BlockSpec(memory_space=pltpu.HBM)
    shapes = [
        jax.ShapeDtypeStruct(shape, dtype) if i < out_hbm else pltpu.VMEM(shape, dtype)
        for i, (shape, dtype) in enumerate(outs)
    ]
    size = sum(math.prod(a.shape) * jnp.dtype(a.dtype).itemsize for a in (*args, *shapes))
    args = [pltpu.with_memory_space_constraint(a, pltpu.HBM) if i in in_hbm else a for i, a in enumerate(args)]
    specs = [smem if a.dtype == jnp.int32 else hbm if i in in_hbm else vmem for i, a in enumerate(args)]
    return pl.pallas_call(
        kernel,
        out_shape=shapes,
        in_specs=specs,
        out_specs=[hbm if i < out_hbm else vmem for i in range(len(shapes))],
        scratch_shapes=list(scratch),
        input_output_aliases=aliases or {},
        compiler_params=pltpu.CompilerParams(vmem_limit_bytes=12 * 1024 * 1024),
        cost_estimate=pl.CostEstimate(flops=int(flops * COST), bytes_accessed=int(size * COST), transcendentals=0),
    )(*args)


def send_kernel(key_ref, k_hbm, v_hbm, out_ref, theirs_ref, mine_ref, sems):
    key = key_ref[0]
    half = out_ref.shape[0]
    copies = []
    for part, ref in enumerate((theirs_ref, mine_ref)):
        for at, hbm in enumerate((k_hbm, v_hbm)):
            copies.append(pltpu.make_async_copy(hbm.at[:, half_of(key, half, part)], ref.at[at], sems.at[part, at]))
            copies[-1].start()
    for copy in copies[:2]:
        copy.wait()
    for j in range(half):
        cols = half_columns(j, key, half)
        out_ref[j] = dot(theirs_ref[0, :, cols], theirs_ref[1, :, cols], 0, 0).astype(BF16)
    for copy in copies[2:]:
        copy.wait()


def own_kernel(key_ref, kv_ref, out_ref):
    key = key_ref[0]
    half = out_ref.shape[0]
    for j in range(half):
        cols = half_columns(j, key, half)
        out_ref[j] = dot(kv_ref[0, :, cols], kv_ref[1, :, cols], 0, 0).astype(BF16)


def fetch_kernel(half, key_ref, q_hbm, g_hbm, theirs_ref, mine_ref, sems):
    key = key_ref[0]
    copies = []
    for part, ref in enumerate((theirs_ref, mine_ref)):
        for at, hbm in enumerate((q_hbm, g_hbm)):
            copies.append(pltpu.make_async_copy(hbm.at[:, half_of(key, half, part)], ref.at[at], sems.at[part, at]))
            copies[-1].start()
    for copy in copies:
        copy.wait()


def half_of(key, half, mine):
    first = key & half
    if not mine:
        first = half ^ first
    return pl.ds(pl.multiple_of(first * HD, half * HD), half * HD)


def half_columns(slot, key, half):
    return pl.ds(pl.multiple_of(((slot ^ key) & (half - 1)) * HD, HD), HD)


def local_kernel(key_ref, kv_ref, qg_ref, their_kv_ref, their_qg_ref, mixed_ref, their_mixed_ref):
    key = key_ref[0]
    half = mixed_ref.shape[0]
    low = triangle(mixed_ref.shape[1], True)
    for j in range(half):
        cols = half_columns(j, key, half)
        for kv, qg, out in ((their_kv_ref, their_qg_ref, their_mixed_ref), (kv_ref, qg_ref, mixed_ref)):
            scores = jnp.where(low, dot(qg[0, :, cols], kv[0, :, cols], 1, 1), 0.0).astype(BF16)
            out[j] = dot(scores, kv[1, :, cols], 1, 0).astype(out.dtype)


def norm_kernel(base, key_ref, qg_ref, their_qg_ref, mixed_ref, their_mixed_ref, mine_ref, theirs_ref, att_ref, gm_ref, state_ref, pack_ref, their_state_ref):
    key = key_ref[0]
    half, rows = mixed_ref.shape[:2]
    for j in range(mine_ref.shape[0]):
        cols = half_columns(base + j, key, half)
        for at, (qg, own_part, e) in enumerate(((qg_ref, mixed_ref, mine_ref), (their_qg_ref, their_mixed_ref, theirs_ref))):
            q = qg[0, :, cols]
            mixed = own_part[base + j] + dot(q, e[j], 1, 0)
            inv_rms = lax.rsqrt(jnp.mean(mixed * mixed, axis=-1, keepdims=True) + 1.0)
            normed = mixed * inv_rms
            g = qg[1, :, cols].astype(F32)
            gm = ((g - normed * jnp.mean(g * normed, axis=-1, keepdims=True)) * inv_rms).astype(BF16)
            state = dot(q, gm, 0, 0).astype(BF16)
            if at:
                pack_ref[j, :rows] = normed.astype(BF16)
                pack_ref[j, rows : 2 * rows] = gm
                pack_ref[j, 2 * rows :] = e[j]
                their_state_ref[j] = state
            else:
                att_ref[j] = normed.astype(BF16)
                gm_ref[j] = gm
                state_ref[j] = state


def grads_kernel(base, per_group, key_ref, q_ref, k_ref, v_ref, *refs):
    att_hbm, gq_hbm, kl_ref, vl_ref, gq_buf, sems = refs[-6:]
    key = key_ref[0]
    rows = q_ref.shape[0]
    low = triangle(rows, True)
    high = triangle(rows, False)
    slots = []
    for at in range(0, per_group * len(GROUPS), per_group):
        group = refs[at : at + per_group]
        for i in range(group[0].shape[0]):
            if per_group == 1:
                slots.append([group[0].at[i, pl.ds(start, n)] for start, n in ((0, rows), (rows, rows), (2 * rows, HD))])
            else:
                slots.append([ref.at[i] for ref in group])
    copies = []
    for j, (att, gm_ref, e_ref) in enumerate(slots):
        cols = columns(base + j, key)
        copies.append(pltpu.make_async_copy(att, att_hbm.at[:, cols], sems.at[0, j]))
        copies[-1].start()
        q = q_ref[:, cols]
        k = k_ref[:, cols]
        v = v_ref[:, cols]
        gm = gm_ref[...]
        gs = jnp.where(low, dot(gm, v, 1, 1), 0.0).astype(BF16)
        gq_buf[j] = (dot(gs, k, 1, 0) + dot(gm, e_ref[...], 1, 1)).astype(BF16)
        copies.append(pltpu.make_async_copy(gq_buf.at[j], gq_hbm.at[:, cols], sems.at[1, j]))
        copies[-1].start()
        gs_turned = jnp.where(high, dot(v, gm, 1, 1), 0.0).astype(BF16)
        kl_ref[j] = dot(gs_turned, q, 1, 0).astype(BF16)
        scores = jnp.where(high, dot(k, q, 1, 1), 0.0).astype(BF16)
        vl_ref[j] = dot(scores, gm, 1, 0).astype(BF16)
    for copy in copies:
        copy.wait()


def last_kernel(base, key_ref, k_ref, v_ref, kl_ref, vl_ref, l_ref, *refs):
    gk_hbm, gv_hbm, gk_buf, gv_buf, sems = refs[-5:]
    key = key_ref[0]
    copies = []
    for j in range(l_ref.shape[0]):
        cols = columns(base + j, key)
        later = l_ref[j]
        gk_buf[j] = (kl_ref[j] + dot(v_ref[:, cols], later, 1, 1)).astype(BF16)
        copies.append(pltpu.make_async_copy(gk_buf.at[j], gk_hbm.at[:, cols], sems.at[0, j]))
        copies[-1].start()
        gv_buf[j] = (vl_ref[j] + dot(k_ref[:, cols], later, 1, 0)).astype(BF16)
        copies.append(pltpu.make_async_copy(gv_buf.at[j], gv_hbm.at[:, cols], sems.at[1, j]))
        copies[-1].start()
    for copy in copies:
        copy.wait()


def swap(array, mask, count):
    return lax.ppermute(array, AXES, [(i, i ^ mask) for i in range(count)])


def exchange_levels(count):
    bits = count.bit_length() - 1
    levels = []
    bit = 3
    while bit < bits:
        first = (1 << bit) | 1
        if bit + 1 < bits:
            second = 1 << (bit + 1)
            levels.append(((3 << bit), (1 << bit) | 1, (2 << bit) | 1))
        else:
            levels.append((first,))
        bit += 2
    return levels


ORDER = (1, 2, 3)
FORWARD = (2, 1, 0)
SCATTER = (3, 4, 7)


GROUPS = ((0, 1), (2, 3))


def slot_key(place, count):
    bits = count.bit_length() - 1
    half = (place ^ (place >> 1)) & 1
    for bit in range(3, bits, 2):
        half = half ^ ((place >> (bit + 0)) ^ (place >> (bit + 1))) & 1
    return (half << 2) | ((place >> 1) & 3)


def beside(arrays, work, tie):
    if work is None:
        return arrays, None
    done = work(tie)
    return lax.optimization_barrier((arrays, done))


def pick(condition, array):
    return jnp.where(condition, array, 0.0)


def tie_to(array, other):
    return lax.optimization_barrier((array, other))[0]


def merge(own, from_core, place, count, backward, works):
    def before(a, b):
        return (a > b) if backward else (a < b)

    chip = place >> 1
    total = [a.astype(F32) + b.astype(F32) for a, b in zip(own, from_core)]
    rounded = [t.astype(BF16) for t in total]
    arrived = {j: swap(rounded[j], SCATTER[j - 1], count) for j in ORDER}
    arrived = [arrived[j] for j in (1, 2, 3)]
    if works[0] is not None and works[0][1]:
        first = works[0][0](arrived[ORDER[0] - 1])
    else:
        arrived, first = beside(arrived, works[0] and works[0][0], rounded[ORDER[0]])
    parts = [total[0], *(a.astype(F32) for a in arrived)]
    cluster = parts[0] + parts[1] + parts[2] + parts[3]
    entering = jnp.zeros_like(cluster)
    second = None
    for at, masks in enumerate(exchange_levels(count)):
        rounded = cluster.astype(BF16)
        if not backward and len(masks) == 3:
            masks = [masks[i] for i in FORWARD]
        arrived = [swap(rounded, mask, count) for mask in masks]
        if at == 0:
            arrived, second = beside(arrived, works[1], rounded)
        for mask, array in zip(masks, arrived):
            array = array.astype(F32)
            entering = entering + pick(before(chip ^ (mask >> 1), chip), array)
            cluster = cluster + array
    low = chip & 3
    sums = []
    for j in range(4):
        value = entering
        for i in range(4):
            if i != j:
                value = value + pick(before(low ^ i, low ^ j), parts[i])
        sums.append(value)
    rounded = [value.astype(BF16) for value in sums]
    arrived = {j: swap(rounded[j], SCATTER[j - 1], count) for j in ORDER}
    arrived = [arrived[j] for j in (1, 2, 3)]
    arrived, third = beside(arrived, works[2], rounded[1])
    return [sums[0], *arrived], (first, second, third)


def share(slots, entering, own, from_core, place, backward):
    first = (place & 1) == (1 if backward else 0)
    entering = jnp.stack([e.astype(F32) for e in entering])
    mine = entering + pick(~first, jnp.stack([from_core[j].astype(F32) for j in slots]))
    theirs = entering + pick(first, jnp.stack([own[j].astype(F32) for j in slots]))
    return mine.astype(BF16), theirs.astype(BF16)


def body(query_rows, key_rows, value_rows, grad_out):
    rows, width = query_rows.shape
    heads = width // HD
    half = heads // 2
    count = lax.axis_size("grp") * lax.axis_size("shard")
    place = lax.axis_index(AXES)
    key = slot_key(place, count).astype(jnp.int32).reshape(1)
    work = rows * width * HD
    scores = rows * width * rows
    block = (half, rows, HD)
    flat = (rows, width)
    dma = pltpu.SemaphoreType.DMA((2, half))
    buffer = pltpu.VMEM(block, BF16)

    def tied(tie):
        return lax.optimization_barrier((key, tie))[0]

    wide = (2, rows, width // 2)
    pairs = pltpu.SemaphoreType.DMA((2, 2))
    send, kv_send, kv_own = call(
        send_kernel, [((half, HD, HD), BF16), (wide, BF16), (wide, BF16)], (key, key_rows, value_rows),
        work, in_hbm=(1, 2), scratch=(pairs,),
    )
    (own,) = call(own_kernel, [((half, HD, HD), BF16)], (tied(send), kv_own), work)
    from_core = swap(send, 1, count)
    def ready(tie):
        qg_send, qg_own = call(
            functools.partial(fetch_kernel, half), [(wide, BF16), (wide, BF16)],
            (tied(tie), query_rows, grad_out), 0, in_hbm=(1, 2), scratch=(pairs,),
        )
        mixed, mixed_send = call(
            local_kernel, [(block, F32), (block, F32)], (key, kv_own, qg_own, kv_send, qg_send), 4 * scores,
        )
        return qg_own, mixed, qg_send, mixed_send

    entering, ((qg_own, mixed, qg_send, mixed_send), _, _) = merge(
        own, from_core, place, count, False, ((ready, False), None, None)
    )
    qg = swap(qg_send, 1, count)
    their_mixed = swap(mixed_send, 1, count)

    def norm(slot, mine, theirs):
        n = mine.shape[0]
        rows_of = (n, rows, HD)
        states = (n, HD, HD)
        return call(
            functools.partial(norm_kernel, slot),
            [(rows_of, BF16), (rows_of, BF16), (states, BF16), ((n, 2 * rows + HD, HD), BF16), (states, BF16)],
            (key, qg_own, qg, mixed, their_mixed, mine, theirs), n * work // 2,
        )

    inner, outer = [], []
    own_back, core_back = [], []
    for at, group in enumerate(GROUPS):
        come = [entering[j] for j in group]
        if at:
            come = tie_to(come, state)
        mine, theirs = share(group, come, own, from_core, place, False)
        att, gm, state, pack, their_state = norm(group[0], mine, theirs)
        inner.append((att, gm, mine))
        outer.append(pack)
        own_back += [state[i] for i in range(len(group))]
        core_back += [their_state[i] for i in range(len(group))]

    late_q, late_k, late_v = tie_to((query_rows, key_rows, value_rows), mixed)

    def grads(base, key, parts, outs):
        per_group = len(parts[0])
        n = 4 + per_group * len(parts)
        return call(
            functools.partial(grads_kernel, base, per_group),
            [(flat, BF16), (flat, BF16), (block, BF16), (block, BF16)],
            (key, late_q, late_k, late_v, *itertools.chain(*parts), *outs),
            4 * scores + work, out_hbm=2, in_hbm=(n, n + 1), scratch=(buffer, dma),
            aliases={n: 0, n + 1: 1} if outs else None,
        )

    made = []

    def grads_first(tie):
        made.append(grads(0, tied(tie), inner, ()))
        return made[0]

    came = []

    def trade(tie):
        came.extend((swap(tie_to(pack, tie), 1, count),) for pack in outer)
        return ()

    def grads_second(tie):
        return grads(half, tied(tie), came, made[0][:2])

    entering, ((_, _, kl_mine, vl_mine), _, (attended, grad_query, kl_other, vl_other)) = merge(
        own_back, core_back, place, count, True, ((grads_first, False), trade, grads_second)
    )
    l_mine, theirs = share(range(half), entering, own_back, core_back, place, True)
    l_other = swap(theirs, 1, count)

    def last(base, key, kl, vl, later, outs):
        n = 6
        return call(
            functools.partial(last_kernel, base),
            [(flat, BF16), (flat, BF16)],
            (key, late_k, late_v, kl, vl, later, *outs),
            2 * work, out_hbm=2, in_hbm=(n, n + 1), scratch=(buffer, buffer, dma),
            aliases={n: 0, n + 1: 1} if outs else None,
        )

    outs = last(0, key, kl_mine, vl_mine, l_mine, ())
    grad_key, grad_value = last(half, key, kl_other, vl_other, l_other, outs)
    return attended, grad_query, grad_key, grad_value


def solution(mesh):
    spec = P(AXES, None)
    return jax.shard_map(
        body, mesh=mesh, in_specs=(spec,) * 4, out_specs=(spec,) * 4, check_vma=False
    )
```

```python
import functools
import itertools
import math

import jax
import jax.numpy as jnp
from jax import lax
from jax.experimental import pallas as pl
from jax.experimental.pallas import tpu as pltpu
from jax.sharding import PartitionSpec as P

HD = 128
COST = 3
AXES = ("grp", "shard")
F32 = jnp.float32
BF16 = jnp.bfloat16


def dot(a, b, a_dim, b_dim):
    return lax.dot_general(a, b, (((a_dim,), (b_dim,)), ((), ())), preferred_element_type=F32)


def columns(slot, key):
    return pl.ds(pl.multiple_of((slot ^ key) * HD, HD), HD)


def triangle(rows, keep_lower):
    at_row = lax.broadcasted_iota(jnp.int32, (rows, rows), 0)
    at_col = lax.broadcasted_iota(jnp.int32, (rows, rows), 1)
    return at_row >= at_col if keep_lower else at_row <= at_col


def call(kernel, outs, args, flops, out_hbm=0, in_hbm=(), scratch=(), aliases=None):
    smem = pl.BlockSpec(memory_space=pltpu.SMEM)
    vmem = pl.BlockSpec(memory_space=pltpu.VMEM)
    hbm = pl.BlockSpec(memory_space=pltpu.HBM)
    shapes = [
        jax.ShapeDtypeStruct(shape, dtype) if i < out_hbm else pltpu.VMEM(shape, dtype)
        for i, (shape, dtype) in enumerate(outs)
    ]
    size = sum(math.prod(a.shape) * jnp.dtype(a.dtype).itemsize for a in (*args, *shapes))
    args = [pltpu.with_memory_space_constraint(a, pltpu.HBM) if i in in_hbm else a for i, a in enumerate(args)]
    specs = [smem if a.dtype == jnp.int32 else hbm if i in in_hbm else vmem for i, a in enumerate(args)]
    return pl.pallas_call(
        kernel,
        out_shape=shapes,
        in_specs=specs,
        out_specs=[hbm if i < out_hbm else vmem for i in range(len(shapes))],
        scratch_shapes=list(scratch),
        input_output_aliases=aliases or {},
        compiler_params=pltpu.CompilerParams(vmem_limit_bytes=12 * 1024 * 1024),
        cost_estimate=pl.CostEstimate(flops=int(flops * COST), bytes_accessed=int(size * COST), transcendentals=0),
    )(*args)


def send_kernel(key_ref, k_hbm, v_hbm, out_ref, theirs_ref, mine_ref, sems):
    key = key_ref[0]
    half = out_ref.shape[0]
    copies = []
    for part, ref in enumerate((theirs_ref, mine_ref)):
        for at, hbm in enumerate((k_hbm, v_hbm)):
            copies.append(pltpu.make_async_copy(hbm.at[:, half_of(key, half, part)], ref.at[at], sems.at[part, at]))
            copies[-1].start()
    for copy in copies[:2]:
        copy.wait()
    for j in range(half):
        cols = half_columns(j, key, half)
        out_ref[j] = dot(theirs_ref[0, :, cols], theirs_ref[1, :, cols], 0, 0).astype(BF16)
    for copy in copies[2:]:
        copy.wait()


def own_kernel(key_ref, kv_ref, out_ref):
    key = key_ref[0]
    half = out_ref.shape[0]
    for j in range(half):
        cols = half_columns(j, key, half)
        out_ref[j] = dot(kv_ref[0, :, cols], kv_ref[1, :, cols], 0, 0).astype(BF16)


def fetch_kernel(half, key_ref, q_hbm, g_hbm, theirs_ref, mine_ref, sems):
    key = key_ref[0]
    copies = []
    for part, ref in enumerate((theirs_ref, mine_ref)):
        for at, hbm in enumerate((q_hbm, g_hbm)):
            copies.append(pltpu.make_async_copy(hbm.at[:, half_of(key, half, part)], ref.at[at], sems.at[part, at]))
            copies[-1].start()
    for copy in copies:
        copy.wait()


def half_of(key, half, mine):
    first = key & half
    if not mine:
        first = half ^ first
    return pl.ds(pl.multiple_of(first * HD, half * HD), half * HD)


def half_columns(slot, key, half):
    return pl.ds(pl.multiple_of(((slot ^ key) & (half - 1)) * HD, HD), HD)


def local_kernel(key_ref, kv_ref, qg_ref, their_kv_ref, their_qg_ref, mixed_ref, their_mixed_ref):
    key = key_ref[0]
    half = mixed_ref.shape[0]
    low = triangle(mixed_ref.shape[1], True)
    for j in range(half):
        cols = half_columns(j, key, half)
        for kv, qg, out in ((their_kv_ref, their_qg_ref, their_mixed_ref), (kv_ref, qg_ref, mixed_ref)):
            scores = jnp.where(low, dot(qg[0, :, cols], kv[0, :, cols], 1, 1), 0.0).astype(BF16)
            out[j] = dot(scores, kv[1, :, cols], 1, 0).astype(out.dtype)


def norm_kernel(base, key_ref, qg_ref, their_qg_ref, mixed_ref, their_mixed_ref, mine_ref, theirs_ref, att_ref, gm_ref, state_ref, pack_ref, their_state_ref):
    key = key_ref[0]
    half, rows = mixed_ref.shape[:2]
    for j in range(mine_ref.shape[0]):
        cols = half_columns(base + j, key, half)
        for at, (qg, own_part, e) in enumerate(((qg_ref, mixed_ref, mine_ref), (their_qg_ref, their_mixed_ref, theirs_ref))):
            q = qg[0, :, cols]
            mixed = own_part[base + j] + dot(q, e[j], 1, 0)
            inv_rms = lax.rsqrt(jnp.mean(mixed * mixed, axis=-1, keepdims=True) + 1.0)
            normed = mixed * inv_rms
            g = qg[1, :, cols].astype(F32)
            gm = ((g - normed * jnp.mean(g * normed, axis=-1, keepdims=True)) * inv_rms).astype(BF16)
            state = dot(q, gm, 0, 0).astype(BF16)
            if at:
                pack_ref[j, :rows] = normed.astype(BF16)
                pack_ref[j, rows : 2 * rows] = gm
                pack_ref[j, 2 * rows :] = e[j]
                their_state_ref[j] = state
            else:
                att_ref[j] = normed.astype(BF16)
                gm_ref[j] = gm
                state_ref[j] = state


def grads_kernel(base, per_group, key_ref, q_ref, k_ref, v_ref, *refs):
    att_hbm, gq_hbm, kl_ref, vl_ref, gq_buf, sems = refs[-6:]
    key = key_ref[0]
    rows = q_ref.shape[0]
    low = triangle(rows, True)
    high = triangle(rows, False)
    slots = []
    for at in range(0, per_group * len(GROUPS), per_group):
        group = refs[at : at + per_group]
        for i in range(group[0].shape[0]):
            if per_group == 1:
                slots.append([group[0].at[i, pl.ds(start, n)] for start, n in ((0, rows), (rows, rows), (2 * rows, HD))])
            else:
                slots.append([ref.at[i] for ref in group])
    copies = []
    for j, (att, gm_ref, e_ref) in enumerate(slots):
        cols = columns(base + j, key)
        copies.append(pltpu.make_async_copy(att, att_hbm.at[:, cols], sems.at[0, j]))
        copies[-1].start()
        q = q_ref[:, cols]
        k = k_ref[:, cols]
        v = v_ref[:, cols]
        gm = gm_ref[...]
        gs = jnp.where(low, dot(gm, v, 1, 1), 0.0).astype(BF16)
        gq_buf[j] = (dot(gs, k, 1, 0) + dot(gm, e_ref[...], 1, 1)).astype(BF16)
        copies.append(pltpu.make_async_copy(gq_buf.at[j], gq_hbm.at[:, cols], sems.at[1, j]))
        copies[-1].start()
        gs_turned = jnp.where(high, dot(v, gm, 1, 1), 0.0).astype(BF16)
        kl_ref[j] = dot(gs_turned, q, 1, 0).astype(BF16)
        scores = jnp.where(high, dot(k, q, 1, 1), 0.0).astype(BF16)
        vl_ref[j] = dot(scores, gm, 1, 0).astype(BF16)
    for copy in copies:
        copy.wait()


def last_kernel(base, key_ref, k_ref, v_ref, kl_ref, vl_ref, l_ref, *refs):
    gk_hbm, gv_hbm, gk_buf, gv_buf, sems = refs[-5:]
    key = key_ref[0]
    copies = []
    for j in range(l_ref.shape[0]):
        cols = columns(base + j, key)
        later = l_ref[j]
        gk_buf[j] = (kl_ref[j] + dot(v_ref[:, cols], later, 1, 1)).astype(BF16)
        copies.append(pltpu.make_async_copy(gk_buf.at[j], gk_hbm.at[:, cols], sems.at[0, j]))
        copies[-1].start()
        gv_buf[j] = (vl_ref[j] + dot(k_ref[:, cols], later, 1, 0)).astype(BF16)
        copies.append(pltpu.make_async_copy(gv_buf.at[j], gv_hbm.at[:, cols], sems.at[1, j]))
        copies[-1].start()
    for copy in copies:
        copy.wait()


def swap(array, mask, count):
    return lax.ppermute(array, AXES, [(i, i ^ mask) for i in range(count)])


def exchange_levels(count):
    bits = count.bit_length() - 1
    levels = []
    bit = 3
    while bit < bits:
        first = (1 << bit) | 1
        if bit + 1 < bits:
            second = 1 << (bit + 1)
            levels.append(((3 << bit) | 1, (1 << bit) | 1, (2 << bit)))
        else:
            levels.append((first,))
        bit += 2
    return levels


ORDER = (1, 2, 3)
FORWARD = (2, 1, 0)
SCATTER = (3, 4, 7)


GROUPS = ((0, 1), (2, 3))


def slot_key(place, count):
    bits = count.bit_length() - 1
    half = (place ^ (place >> 1)) & 1
    for bit in range(3, bits, 2):
        half = half ^ (place >> bit) & 1
    return (half << 2) | ((place >> 1) & 3)


def beside(arrays, work, tie):
    if work is None:
        return arrays, None
    done = work(tie)
    return lax.optimization_barrier((arrays, done))


def pick(condition, array):
    return jnp.where(condition, array, 0.0)


def tie_to(array, other):
    return lax.optimization_barrier((array, other))[0]


def merge(own, from_core, place, count, backward, works):
    def before(a, b):
        return (a > b) if backward else (a < b)

    chip = place >> 1
    total = [a.astype(F32) + b.astype(F32) for a, b in zip(own, from_core)]
    rounded = [t.astype(BF16) for t in total]
    arrived = {j: swap(rounded[j], SCATTER[j - 1], count) for j in ORDER}
    arrived = [arrived[j] for j in (1, 2, 3)]
    if works[0] is not None and works[0][1]:
        first = works[0][0](arrived[ORDER[0] - 1])
    else:
        arrived, first = beside(arrived, works[0] and works[0][0], rounded[ORDER[0]])
    parts = [total[0], *(a.astype(F32) for a in arrived)]
    cluster = parts[0] + parts[1] + parts[2] + parts[3]
    entering = jnp.zeros_like(cluster)
    second = None
    for at, masks in enumerate(exchange_levels(count)):
        rounded = cluster.astype(BF16)
        if not backward and len(masks) == 3:
            masks = [masks[i] for i in FORWARD]
        arrived = [swap(rounded, mask, count) for mask in masks]
        if at == 0:
            arrived, second = beside(arrived, works[1], rounded)
        for mask, array in zip(masks, arrived):
            array = array.astype(F32)
            entering = entering + pick(before(chip ^ (mask >> 1), chip), array)
            cluster = cluster + array
    low = chip & 3
    sums = []
    for j in range(4):
        value = entering
        for i in range(4):
            if i != j:
                value = value + pick(before(low ^ i, low ^ j), parts[i])
        sums.append(value)
    rounded = [value.astype(BF16) for value in sums]
    arrived = {j: swap(rounded[j], SCATTER[j - 1], count) for j in ORDER}
    arrived = [arrived[j] for j in (1, 2, 3)]
    arrived, third = beside(arrived, works[2], rounded[1])
    return [sums[0], *arrived], (first, second, third)


def share(slots, entering, own, from_core, place, backward):
    first = (place & 1) == (1 if backward else 0)
    entering = jnp.stack([e.astype(F32) for e in entering])
    mine = entering + pick(~first, jnp.stack([from_core[j].astype(F32) for j in slots]))
    theirs = entering + pick(first, jnp.stack([own[j].astype(F32) for j in slots]))
    return mine.astype(BF16), theirs.astype(BF16)


def body(query_rows, key_rows, value_rows, grad_out):
    rows, width = query_rows.shape
    heads = width // HD
    half = heads // 2
    count = lax.axis_size("grp") * lax.axis_size("shard")
    place = lax.axis_index(AXES)
    key = slot_key(place, count).astype(jnp.int32).reshape(1)
    work = rows * width * HD
    scores = rows * width * rows
    block = (half, rows, HD)
    flat = (rows, width)
    dma = pltpu.SemaphoreType.DMA((2, half))
    buffer = pltpu.VMEM(block, BF16)

    def tied(tie):
        return lax.optimization_barrier((key, tie))[0]

    wide = (2, rows, width // 2)
    pairs = pltpu.SemaphoreType.DMA((2, 2))
    send, kv_send, kv_own = call(
        send_kernel, [((half, HD, HD), BF16), (wide, BF16), (wide, BF16)], (key, key_rows, value_rows),
        work, in_hbm=(1, 2), scratch=(pairs,),
    )
    (own,) = call(own_kernel, [((half, HD, HD), BF16)], (tied(send), kv_own), work)
    from_core = swap(send, 1, count)
    def ready(tie):
        qg_send, qg_own = call(
            functools.partial(fetch_kernel, half), [(wide, BF16), (wide, BF16)],
            (tied(tie), query_rows, grad_out), 0, in_hbm=(1, 2), scratch=(pairs,),
        )
        mixed, mixed_send = call(
            local_kernel, [(block, F32), (block, F32)], (key, kv_own, qg_own, kv_send, qg_send), 4 * scores,
        )
        return qg_own, mixed, qg_send, mixed_send

    entering, ((qg_own, mixed, qg_send, mixed_send), _, _) = merge(
        own, from_core, place, count, False, ((ready, False), None, None)
    )
    qg = swap(qg_send, 1, count)
    their_mixed = swap(mixed_send, 1, count)

    def norm(slot, mine, theirs):
        n = mine.shape[0]
        rows_of = (n, rows, HD)
        states = (n, HD, HD)
        return call(
            functools.partial(norm_kernel, slot),
            [(rows_of, BF16), (rows_of, BF16), (states, BF16), ((n, 2 * rows + HD, HD), BF16), (states, BF16)],
            (key, qg_own, qg, mixed, their_mixed, mine, theirs), n * work // 2,
        )

    inner, outer = [], []
    own_back, core_back = [], []
    for at, group in enumerate(GROUPS):
        come = [entering[j] for j in group]
        if at:
            come = tie_to(come, state)
        mine, theirs = share(group, come, own, from_core, place, False)
        att, gm, state, pack, their_state = norm(group[0], mine, theirs)
        inner.append((att, gm, mine))
        outer.append(pack)
        own_back += [state[i] for i in range(len(group))]
        core_back += [their_state[i] for i in range(len(group))]

    late_q, late_k, late_v = tie_to((query_rows, key_rows, value_rows), mixed)

    def grads(base, key, parts, outs):
        per_group = len(parts[0])
        n = 4 + per_group * len(parts)
        return call(
            functools.partial(grads_kernel, base, per_group),
            [(flat, BF16), (flat, BF16), (block, BF16), (block, BF16)],
            (key, late_q, late_k, late_v, *itertools.chain(*parts), *outs),
            4 * scores + work, out_hbm=2, in_hbm=(n, n + 1), scratch=(buffer, dma),
            aliases={n: 0, n + 1: 1} if outs else None,
        )

    made = []

    def grads_first(tie):
        made.append(grads(0, tied(tie), inner, ()))
        return made[0]

    came = []

    def trade(tie):
        came.extend((swap(tie_to(pack, tie), 1, count),) for pack in outer)
        return ()

    def grads_second(tie):
        return grads(half, tied(tie), came, made[0][:2])

    entering, ((_, _, kl_mine, vl_mine), _, (attended, grad_query, kl_other, vl_other)) = merge(
        own_back, core_back, place, count, True, ((grads_first, False), trade, grads_second)
    )
    l_mine, theirs = share(range(half), entering, own_back, core_back, place, True)
    l_other = swap(theirs, 1, count)

    def last(base, key, kl, vl, later, outs):
        n = 6
        return call(
            functools.partial(last_kernel, base),
            [(flat, BF16), (flat, BF16)],
            (key, late_k, late_v, kl, vl, later, *outs),
            2 * work, out_hbm=2, in_hbm=(n, n + 1), scratch=(buffer, buffer, dma),
            aliases={n: 0, n + 1: 1} if outs else None,
        )

    outs = last(0, key, kl_mine, vl_mine, l_mine, ())
    grad_key, grad_value = last(half, key, kl_other, vl_other, l_other, outs)
    return attended, grad_query, grad_key, grad_value


def solution(mesh):
    spec = P(AXES, None)
    return jax.shard_map(
        body, mesh=mesh, in_specs=(spec,) * 4, out_specs=(spec,) * 4, check_vma=False
    )
```

```python
import functools
import itertools
import math

import jax
import jax.numpy as jnp
from jax import lax
from jax.experimental import pallas as pl
from jax.experimental.pallas import tpu as pltpu
from jax.sharding import PartitionSpec as P

HD = 128
COST = 3
AXES = ("grp", "shard")
F32 = jnp.float32
BF16 = jnp.bfloat16


def dot(a, b, a_dim, b_dim):
    return lax.dot_general(a, b, (((a_dim,), (b_dim,)), ((), ())), preferred_element_type=F32)


def columns(slot, key):
    return pl.ds(pl.multiple_of((slot ^ key) * HD, HD), HD)


def triangle(rows, keep_lower):
    at_row = lax.broadcasted_iota(jnp.int32, (rows, rows), 0)
    at_col = lax.broadcasted_iota(jnp.int32, (rows, rows), 1)
    return at_row >= at_col if keep_lower else at_row <= at_col


def call(kernel, outs, args, flops, out_hbm=0, in_hbm=(), scratch=(), aliases=None):
    smem = pl.BlockSpec(memory_space=pltpu.SMEM)
    vmem = pl.BlockSpec(memory_space=pltpu.VMEM)
    hbm = pl.BlockSpec(memory_space=pltpu.HBM)
    shapes = [
        jax.ShapeDtypeStruct(shape, dtype) if i < out_hbm else pltpu.VMEM(shape, dtype)
        for i, (shape, dtype) in enumerate(outs)
    ]
    size = sum(math.prod(a.shape) * jnp.dtype(a.dtype).itemsize for a in (*args, *shapes))
    args = [pltpu.with_memory_space_constraint(a, pltpu.HBM) if i in in_hbm else a for i, a in enumerate(args)]
    specs = [smem if a.dtype == jnp.int32 else hbm if i in in_hbm else vmem for i, a in enumerate(args)]
    return pl.pallas_call(
        kernel,
        out_shape=shapes,
        in_specs=specs,
        out_specs=[hbm if i < out_hbm else vmem for i in range(len(shapes))],
        scratch_shapes=list(scratch),
        input_output_aliases=aliases or {},
        compiler_params=pltpu.CompilerParams(vmem_limit_bytes=12 * 1024 * 1024),
        cost_estimate=pl.CostEstimate(flops=int(flops * COST), bytes_accessed=int(size * COST), transcendentals=0),
    )(*args)


def send_kernel(key_ref, k_hbm, v_hbm, out_ref, theirs_ref, mine_ref, sems):
    key = key_ref[0]
    half = out_ref.shape[0]
    copies = []
    for part, ref in enumerate((theirs_ref, mine_ref)):
        for at, hbm in enumerate((k_hbm, v_hbm)):
            copies.append(pltpu.make_async_copy(hbm.at[:, half_of(key, half, part)], ref.at[at], sems.at[part, at]))
            copies[-1].start()
    for copy in copies[:2]:
        copy.wait()
    for j in range(half):
        cols = half_columns(j, key, half)
        out_ref[j] = dot(theirs_ref[0, :, cols], theirs_ref[1, :, cols], 0, 0).astype(BF16)
    for copy in copies[2:]:
        copy.wait()


def own_kernel(key_ref, kv_ref, out_ref):
    key = key_ref[0]
    half = out_ref.shape[0]
    for j in range(half):
        cols = half_columns(j, key, half)
        out_ref[j] = dot(kv_ref[0, :, cols], kv_ref[1, :, cols], 0, 0).astype(BF16)


def fetch_kernel(half, key_ref, q_hbm, g_hbm, theirs_ref, mine_ref, sems):
    key = key_ref[0]
    copies = []
    for part, ref in enumerate((theirs_ref, mine_ref)):
        for at, hbm in enumerate((q_hbm, g_hbm)):
            copies.append(pltpu.make_async_copy(hbm.at[:, half_of(key, half, part)], ref.at[at], sems.at[part, at]))
            copies[-1].start()
    for copy in copies:
        copy.wait()


def half_of(key, half, mine):
    first = key & half
    if not mine:
        first = half ^ first
    return pl.ds(pl.multiple_of(first * HD, half * HD), half * HD)


def half_columns(slot, key, half):
    return pl.ds(pl.multiple_of(((slot ^ key) & (half - 1)) * HD, HD), HD)


def local_kernel(key_ref, kv_ref, qg_ref, their_kv_ref, their_qg_ref, mixed_ref, their_mixed_ref):
    key = key_ref[0]
    half = mixed_ref.shape[0]
    low = triangle(mixed_ref.shape[1], True)
    for j in range(half):
        cols = half_columns(j, key, half)
        for kv, qg, out in ((their_kv_ref, their_qg_ref, their_mixed_ref), (kv_ref, qg_ref, mixed_ref)):
            scores = jnp.where(low, dot(qg[0, :, cols], kv[0, :, cols], 1, 1), 0.0).astype(BF16)
            out[j] = dot(scores, kv[1, :, cols], 1, 0).astype(out.dtype)


def norm_kernel(base, key_ref, qg_ref, their_qg_ref, mixed_ref, their_mixed_ref, mine_ref, theirs_ref, att_ref, gm_ref, state_ref, pack_ref, their_state_ref):
    key = key_ref[0]
    half, rows = mixed_ref.shape[:2]
    for j in range(mine_ref.shape[0]):
        cols = half_columns(base + j, key, half)
        for at, (qg, own_part, e) in enumerate(((qg_ref, mixed_ref, mine_ref), (their_qg_ref, their_mixed_ref, theirs_ref))):
            q = qg[0, :, cols]
            mixed = own_part[base + j] + dot(q, e[j], 1, 0)
            inv_rms = lax.rsqrt(jnp.mean(mixed * mixed, axis=-1, keepdims=True) + 1.0)
            normed = mixed * inv_rms
            g = qg[1, :, cols].astype(F32)
            gm = ((g - normed * jnp.mean(g * normed, axis=-1, keepdims=True)) * inv_rms).astype(BF16)
            state = dot(q, gm, 0, 0).astype(BF16)
            if at:
                pack_ref[j, :rows] = normed.astype(BF16)
                pack_ref[j, rows : 2 * rows] = gm
                pack_ref[j, 2 * rows :] = e[j]
                their_state_ref[j] = state
            else:
                att_ref[j] = normed.astype(BF16)
                gm_ref[j] = gm
                state_ref[j] = state


def grads_kernel(base, per_group, key_ref, q_ref, k_ref, v_ref, *refs):
    att_hbm, gq_hbm, kl_ref, vl_ref, gq_buf, sems = refs[-6:]
    key = key_ref[0]
    rows = q_ref.shape[0]
    low = triangle(rows, True)
    high = triangle(rows, False)
    slots = []
    for at in range(0, per_group * len(GROUPS), per_group):
        group = refs[at : at + per_group]
        for i in range(group[0].shape[0]):
            if per_group == 1:
                slots.append([group[0].at[i, pl.ds(start, n)] for start, n in ((0, rows), (rows, rows), (2 * rows, HD))])
            else:
                slots.append([ref.at[i] for ref in group])
    copies = []
    for j, (att, gm_ref, e_ref) in enumerate(slots):
        cols = columns(base + j, key)
        copies.append(pltpu.make_async_copy(att, att_hbm.at[:, cols], sems.at[0, j]))
        copies[-1].start()
        q = q_ref[:, cols]
        k = k_ref[:, cols]
        v = v_ref[:, cols]
        gm = gm_ref[...]
        gs = jnp.where(low, dot(gm, v, 1, 1), 0.0).astype(BF16)
        gq_buf[j] = (dot(gs, k, 1, 0) + dot(gm, e_ref[...], 1, 1)).astype(BF16)
        copies.append(pltpu.make_async_copy(gq_buf.at[j], gq_hbm.at[:, cols], sems.at[1, j]))
        copies[-1].start()
        gs_turned = jnp.where(high, dot(v, gm, 1, 1), 0.0).astype(BF16)
        kl_ref[j] = dot(gs_turned, q, 1, 0).astype(BF16)
        scores = jnp.where(high, dot(k, q, 1, 1), 0.0).astype(BF16)
        vl_ref[j] = dot(scores, gm, 1, 0).astype(BF16)
    for copy in copies:
        copy.wait()


def last_kernel(base, key_ref, k_ref, v_ref, kl_ref, vl_ref, l_ref, *refs):
    gk_hbm, gv_hbm, gk_buf, gv_buf, sems = refs[-5:]
    key = key_ref[0]
    copies = []
    for j in range(l_ref.shape[0]):
        cols = columns(base + j, key)
        later = l_ref[j]
        gk_buf[j] = (kl_ref[j] + dot(v_ref[:, cols], later, 1, 1)).astype(BF16)
        copies.append(pltpu.make_async_copy(gk_buf.at[j], gk_hbm.at[:, cols], sems.at[0, j]))
        copies[-1].start()
        gv_buf[j] = (vl_ref[j] + dot(k_ref[:, cols], later, 1, 0)).astype(BF16)
        copies.append(pltpu.make_async_copy(gv_buf.at[j], gv_hbm.at[:, cols], sems.at[1, j]))
        copies[-1].start()
    for copy in copies:
        copy.wait()


def swap(array, mask, count):
    return lax.ppermute(array, AXES, [(i, i ^ mask) for i in range(count)])


def exchange_levels(count):
    bits = count.bit_length() - 1
    levels = []
    bit = 3
    while bit < bits:
        first = (1 << bit) | 1
        if bit + 1 < bits:
            second = 1 << (bit + 1)
            levels.append(((3 << bit) | 1, (1 << bit) | 1, (2 << bit)))
        else:
            levels.append((first,))
        bit += 2
    return levels


ORDER = (1, 2, 3)
FORWARD = (2, 1, 0)
SCATTER = (3, 4, 7)


GROUPS = ((0, 1), (2, 3))


def slot_key(place, count):
    bits = count.bit_length() - 1
    half = (place ^ (place >> 1)) & 1
    for bit in range(3, bits, 2):
        half = half ^ (place >> bit) & 1
    return (half << 2) | ((place >> 1) & 3)


def beside(arrays, work, tie):
    if work is None:
        return arrays, None
    done = work(tie)
    return lax.optimization_barrier((arrays, done))


def pick(condition, array):
    return jnp.where(condition, array, 0.0)


def tie_to(array, other):
    return lax.optimization_barrier((array, other))[0]


def merge(own, from_core, place, count, backward, works):
    def before(a, b):
        return (a > b) if backward else (a < b)

    chip = place >> 1
    total = [a.astype(F32) + b.astype(F32) for a, b in zip(own, from_core)]
    rounded = [t.astype(BF16) for t in total]
    arrived = {j: swap(rounded[j], SCATTER[j - 1], count) for j in ORDER}
    arrived = [arrived[j] for j in (1, 2, 3)]
    if works[0] is not None and works[0][1]:
        first = works[0][0](arrived[ORDER[0] - 1])
    else:
        arrived, first = beside(arrived, works[0] and works[0][0], rounded[ORDER[0]])
    parts = [total[0], *(a.astype(F32) for a in arrived)]
    cluster = parts[0] + parts[1] + parts[2] + parts[3]
    entering = jnp.zeros_like(cluster)
    second = None
    for at, masks in enumerate(exchange_levels(count)):
        rounded = cluster.astype(BF16)
        if not backward and len(masks) == 3:
            masks = [masks[i] for i in FORWARD]
        arrived = [swap(rounded, mask, count) for mask in masks]
        if at == 0:
            arrived, second = beside(arrived, works[1], rounded)
        for mask, array in zip(masks, arrived):
            array = array.astype(F32)
            entering = entering + pick(before(chip ^ (mask >> 1), chip), array)
            cluster = cluster + array
    low = chip & 3
    sums = []
    for j in range(4):
        value = entering
        for i in range(4):
            if i != j:
                value = value + pick(before(low ^ i, low ^ j), parts[i])
        sums.append(value)
    rounded = [value.astype(BF16) for value in sums]
    arrived = {j: swap(rounded[j], SCATTER[j - 1], count) for j in ORDER}
    arrived = [arrived[j] for j in (1, 2, 3)]
    arrived, third = beside(arrived, works[2], rounded[1])
    return [sums[0], *arrived], (first, second, third)


def share(slots, entering, own, from_core, place, backward):
    first = (place & 1) == (1 if backward else 0)
    entering = jnp.stack([e.astype(F32) for e in entering])
    mine = entering + pick(~first, jnp.stack([from_core[j].astype(F32) for j in slots]))
    theirs = entering + pick(first, jnp.stack([own[j].astype(F32) for j in slots]))
    return mine.astype(BF16), theirs.astype(BF16)


def body(query_rows, key_rows, value_rows, grad_out):
    rows, width = query_rows.shape
    heads = width // HD
    half = heads // 2
    count = lax.axis_size("grp") * lax.axis_size("shard")
    place = lax.axis_index(AXES)
    key = slot_key(place, count).astype(jnp.int32).reshape(1)
    work = rows * width * HD
    scores = rows * width * rows
    block = (half, rows, HD)
    flat = (rows, width)
    dma = pltpu.SemaphoreType.DMA((2, half))
    buffer = pltpu.VMEM(block, BF16)

    def tied(tie):
        return lax.optimization_barrier((key, tie))[0]

    wide = (2, rows, width // 2)
    pairs = pltpu.SemaphoreType.DMA((2, 2))
    send, kv_send, kv_own = call(
        send_kernel, [((half, HD, HD), BF16), (wide, BF16), (wide, BF16)], (key, key_rows, value_rows),
        work, in_hbm=(1, 2), scratch=(pairs,),
    )
    (own,) = call(own_kernel, [((half, HD, HD), BF16)], (tied(send), kv_own), work)
    from_core = swap(send, 1, count)
    def ready(tie):
        qg_send, qg_own = call(
            functools.partial(fetch_kernel, half), [(wide, BF16), (wide, BF16)],
            (tied(tie), query_rows, grad_out), 0, in_hbm=(1, 2), scratch=(pairs,),
        )
        mixed, mixed_send = call(
            local_kernel, [(block, F32), (block, F32)], (key, kv_own, qg_own, kv_send, qg_send), 4 * scores,
        )
        return qg_own, mixed, qg_send, mixed_send

    entering, ((qg_own, mixed, qg_send, mixed_send), _, _) = merge(
        own, from_core, place, count, False, ((ready, False), None, None)
    )
    qg = swap(qg_send, 1, count)
    their_mixed = swap(mixed_send, 1, count)

    def norm(slot, mine, theirs):
        n = mine.shape[0]
        rows_of = (n, rows, HD)
        states = (n, HD, HD)
        return call(
            functools.partial(norm_kernel, slot),
            [(rows_of, BF16), (rows_of, BF16), (states, BF16), ((n, 2 * rows + HD, HD), BF16), (states, BF16)],
            (key, qg_own, qg, mixed, their_mixed, mine, theirs), n * work // 2,
        )

    inner, outer = [], []
    own_back, core_back = [], []
    for at, group in enumerate(GROUPS):
        come = [entering[j] for j in group]
        if at:
            come = tie_to(come, state)
        mine, theirs = share(group, come, own, from_core, place, False)
        att, gm, state, pack, their_state = norm(group[0], mine, theirs)
        inner.append((att, gm, mine))
        outer.append(pack)
        own_back += [state[i] for i in range(len(group))]
        core_back += [their_state[i] for i in range(len(group))]

    late_q, late_k, late_v = tie_to((query_rows, key_rows, value_rows), inner[1][2])

    def grads(base, key, parts, outs):
        per_group = len(parts[0])
        n = 4 + per_group * len(parts)
        return call(
            functools.partial(grads_kernel, base, per_group),
            [(flat, BF16), (flat, BF16), (block, BF16), (block, BF16)],
            (key, late_q, late_k, late_v, *itertools.chain(*parts), *outs),
            4 * scores + work, out_hbm=2, in_hbm=(n, n + 1), scratch=(buffer, dma),
            aliases={n: 0, n + 1: 1} if outs else None,
        )

    made = []

    def grads_first(tie):
        made.append(grads(0, tied(tie), inner, ()))
        return made[0]

    came = []

    def trade(tie):
        came.extend((swap(tie_to(pack, tie), 1, count),) for pack in outer)
        return ()

    def grads_second(tie):
        return grads(half, tied(tie), came, made[0][:2])

    entering, ((_, _, kl_mine, vl_mine), _, (attended, grad_query, kl_other, vl_other)) = merge(
        own_back, core_back, place, count, True, ((grads_first, False), trade, grads_second)
    )
    l_mine, theirs = share(range(half), entering, own_back, core_back, place, True)
    l_other = swap(theirs, 1, count)

    def last(base, key, kl, vl, later, outs):
        n = 6
        return call(
            functools.partial(last_kernel, base),
            [(flat, BF16), (flat, BF16)],
            (key, late_k, late_v, kl, vl, later, *outs),
            2 * work, out_hbm=2, in_hbm=(n, n + 1), scratch=(buffer, buffer, dma),
            aliases={n: 0, n + 1: 1} if outs else None,
        )

    outs = last(0, key, kl_mine, vl_mine, l_mine, ())
    grad_key, grad_value = last(half, key, kl_other, vl_other, l_other, outs)
    return attended, grad_query, grad_key, grad_value


def solution(mesh):
    spec = P(AXES, None)
    return jax.shard_map(
        body, mesh=mesh, in_specs=(spec,) * 4, out_specs=(spec,) * 4, check_vma=False
    )
```
